256 devices in a mesh: ctx: 64 (over z, y, core), head: 4 (over x).
Axes of the slice: x: 4, y: 4, z: 8, core: 2. Of those that a mesh axis runs over, the one named last changes fastest.
Arguments:
- inputs: bfloat16 [16384, 8, 1024], P('ctx', None, 'head'), may hold values from -6 to 6
- step_size: float32 [16384, 8, 16], P('ctx', None, 'head'), may hold values from 0.125 to 2
- decay_rate: float32 [8, 16], P(None, 'head'), may hold values from -0.1 to 0
- b_proj: bfloat16 [16384, 8, 128], P('ctx'), may hold values from -6 to 6
- c_proj: bfloat16 [16384, 8, 128], P('ctx'), may hold values from -6 to 6
- grad_out: bfloat16 [16384, 8, 1024], P('ctx', None, 'head'), may hold values from -0.005859375 to 0.005859375
- segment_ids: int32 [16384], P('ctx'), may hold values from 0 to 15, never falling along the last dimension, each value on 1 to 4096 neighbouring positions
Outputs:
- grad_in: bfloat16 [16384, 8, 1024], P('ctx', None, 'head')
- grad_step: float32 [16384, 8, 16], P('ctx', None, 'head')
- grad_b: float32 [16384, 8, 128], P('ctx', 'head')
- grad_c: float32 [16384, 8, 128], P('ctx', 'head')
The draws below stay inside these ranges and needn't reach their ends.
All inputs are finite; a program needn't handle non-finite values.
Results may differ from the reference program's by a relative error of at most 0.001.
Values sent between devices are 32-bit elements; how exact they have to be, the bound alone decides.
No kernel may reach another device: no remote copies, remote signals or barrier semaphores. Data moves between devices by JAX's collectives and lax.ppermute only.
A program may use at most 320 MiB of HBM per device.

```python
import math
import jax
import jax.numpy as jnp
import numpy as np
from jax import lax

HEADS = 128
G = 8
P_SIZE = 64
N = 128
SPAN = 128
TOKENS = 16384


def log_spread(rng_key, shape, lowest, highest):
    return jnp.exp(jax.random.uniform(rng_key, shape, jnp.float32, math.log(lowest), math.log(highest)))


def draw_decay_rate(key, part):
    key = jax.random.fold_in(key, 11)
    sub_keys = jax.random.split(key, 3)
    fast_share = 0.5
    fast_heads = jax.random.uniform(sub_keys[0], (G, HEADS // G), jnp.float32) < fast_share
    fast_rate = log_spread(sub_keys[1], (G, HEADS // G), 0.03, 0.1)
    slow_rate = log_spread(sub_keys[2], (G, HEADS // G), 1.0, 3.5) / TOKENS
    return -jnp.where(fast_heads, fast_rate, jnp.minimum(slow_rate, 0.1))


def draw_step_size(key, part):
    key = jax.random.fold_in(key, 12)
    sub_keys = jax.random.split(key, 2)
    blocks = TOKENS // SPAN
    block_scale = log_spread(sub_keys[0], (blocks, 1, 1), 0.5, 2.0)
    token_scale = log_spread(sub_keys[1], (TOKENS, G, HEADS // G), 0.5, 2.0)
    return 0.5 * jnp.repeat(block_scale, SPAN, axis=0) * token_scale


def levels(own_key, extent, cuts, least, largest):
    loudness, own = 1.0, jax.random.fold_in(own_key, 6)
    for dim, shards_of in cuts:
        draws = jnp.exp(jax.random.uniform(jax.random.fold_in(own, dim), (shards_of,), jnp.float32, least / len(cuts), largest / len(cuts)))
        loudness = loudness * jnp.repeat(draws, extent[dim] // shards_of).reshape([-1 if axis == dim else 1 for axis in range(len(extent))])
    return loudness


def split_up(number_of, total, limit, lean):
    loads = [(1 << 20) // math.isqrt(grade ** lean) + 1 for grade in range(2, number_of + 1)]
    rest, counts = total - limit - (number_of - 1), [1] * (number_of - 1)
    while rest > 0:
        movable = [i for i in range(number_of - 1) if counts[i] < limit]
        mass, budget = sum([loads[i] for i in movable]), rest
        for i in movable:
            extra = min(limit - counts[i], max(1, budget * loads[i] // mass), rest)
            counts[i] = counts[i] + extra
            rest = rest - extra
    return np.array([limit] + counts)


def uneven_parts(stream_key, count, total, limit, skew):
    if count == 2:
        one = jax.random.randint(stream_key, (), max(1, total - limit), min(limit, total - 1) + 1)
        return jnp.stack([one, total - one])
    lengths = jnp.asarray(split_up(count, total, limit, skew), jnp.int32)
    couples = (count - 1) // 2
    giver, receiver = lengths[1:1 + 2 * couples:2], lengths[2:2 + 2 * couples:2]
    margin = jnp.minimum(giver - 1, limit - receiver)
    passed = jax.random.randint(jax.random.fold_in(stream_key, 1), (couples,), 0, 1 << 20) % (margin + 1)
    lengths = lengths.at[1:1 + 2 * couples:2].set(giver - passed).at[2:2 + 2 * couples:2].set(receiver + passed)
    return lengths[jax.random.permutation(jax.random.fold_in(stream_key, 2), count)]


def normal_values(rng, shape, spread, most, shards=(), dtype=jnp.bfloat16):
    values = jax.random.normal(rng, shape, jnp.float32) * spread
    if len(shards) > 0:
        values = levels(rng, shape, shards, -0.22, 0.18) * values
    return jnp.clip(values, min=-most, max=most).astype(dtype)


def setup_inputs(seed: int = 0) -> dict:
    seeds = jax.random.split(jax.random.key(seed), 8)
    inputs = normal_values(seeds[0], (TOKENS, G, HEADS // G * P_SIZE), 1.0, 6.0, ((0, 64), (2, 4)))
    step_size = draw_step_size(jax.random.fold_in(seeds[7], 71), 0)
    decay_rate = draw_decay_rate(jax.random.fold_in(seeds[7], 71), 0)
    b_proj = normal_values(seeds[3], (TOKENS, G, N), 1.0, 6.0, ((0, 64),))
    c_proj = normal_values(seeds[4], (TOKENS, G, N), 1.0, 6.0, ((0, 64),))
    grad_out = normal_values(seeds[5], (TOKENS, G, HEADS // G * P_SIZE), 0.001, 0.005859375, ((0, 64), (2, 4)))
    segment_ids = jnp.searchsorted(jnp.cumsum(uneven_parts(seeds[6], 16, TOKENS, TOKENS // 4, 1)), jnp.arange(TOKENS), side="right").astype(jnp.int32)
    return {"inputs": inputs, "step_size": step_size, "decay_rate": decay_rate, "b_proj": b_proj, "c_proj": c_proj, "grad_out": grad_out, "segment_ids": segment_ids}


PRECISE = lax.Precision.HIGHEST


def product(pattern, first_op, second_op):
    return jnp.einsum(pattern, first_op, second_op, precision=PRECISE)


def span_weights(step_size, decay_rate, segment):
    cumlog = jnp.cumsum(step_size * decay_rate[None], axis=0)
    at_first = (segment == segment[0]).astype(jnp.float32)[:, None, None]
    at_last = (segment == segment[-1]).astype(jnp.float32)[:, None, None]
    alpha_w = jnp.exp(cumlog) * at_first
    beta_w = jnp.exp(cumlog[-1][None] - cumlog) * at_last
    return cumlog, alpha_w, beta_w


def span_summary(inputs, step_size, decay_rate, b_proj, c_proj, grad_out, segment):
    cumlog, alpha_w, beta_w = span_weights(step_size, decay_rate, segment)
    decayed = jnp.exp(cumlog[-1]) * (segment[0] == segment[-1]).astype(jnp.float32)
    forward_sum = product("sgjp,sgn->gjpn", inputs * (beta_w * step_size)[..., None], b_proj)
    reverse_sum = product("rgjp,rgn->gjpn", grad_out * alpha_w[..., None], c_proj)
    return decayed, forward_sum, reverse_sum


def span_grads(inputs, step_size, decay_rate, b_proj, c_proj, grad_out, segment, state_in, adjoint_in):
    length = segment.shape[0]
    cumlog, alpha_w, beta_w = span_weights(step_size, decay_rate, segment)
    row_ids = lax.broadcasted_iota(jnp.int32, (length, length), 0)
    col_ids = lax.broadcasted_iota(jnp.int32, (length, length), 1)
    linked = (segment[:, None] == segment[None, :]) & (row_ids >= col_ids)
    cum_cols = jnp.transpose(cumlog, (1, 2, 0))
    differ = cum_cols[:, :, :, None] - cum_cols[:, :, None, :]
    decays = jnp.where(linked[None, None], jnp.exp(jnp.minimum(differ, 0.0)), 0.0)
    upper_tri = (row_ids <= col_ids).astype(jnp.float32)
    lower_tri = (row_ids >= col_ids).astype(jnp.float32)
    step_cols = jnp.transpose(step_size, (1, 2, 0))
    cross_dx = product("tgjp,sgjp->gjts", grad_out, inputs)
    cross_cb = product("tgn,sgn->gts", c_proj, b_proj)
    weighted = decays * cross_dx * step_cols[:, :, None, :]
    summed = jnp.sum(weighted, axis=1)
    dy_state = product("tgjp,gjpn->tgjn", grad_out, state_in)
    x_adjoint = product("sgjp,gjpn->sgjn", inputs, adjoint_in)
    grad_c = product("gts,sgn->tgn", summed, b_proj) + jnp.sum(alpha_w[..., None] * dy_state, axis=2)
    grad_b = product("gts,tgn->sgn", summed, c_proj) + jnp.sum((step_size * beta_w)[..., None] * x_adjoint, axis=2)
    raw_dx = product("gjrt,rgjp->tgjp", decays * cross_cb[:, None], grad_out)
    raw_dx = raw_dx + beta_w[..., None] * product("tgn,gjpn->tgjp", b_proj, adjoint_in)
    running = product("gjrs,st->gjrt", weighted * cross_cb[:, None], upper_tri)
    term_four = jnp.transpose(jnp.sum(running * lower_tri[None, None], axis=2), (2, 0, 1))
    term_one = alpha_w * beta_w * jnp.sum(state_in * adjoint_in, axis=(2, 3))[None]
    dy_c = jnp.sum(dy_state * c_proj[:, :, None, :], axis=3)
    term_two = alpha_w * product("gjrt,rgj->tgj", decays, dy_c)
    x_b = step_size * jnp.sum(x_adjoint * b_proj[:, :, None, :], axis=3)
    term_three = beta_w * product("gjts,sgj->tgj", decays, x_b)
    along_x = jnp.sum(inputs * raw_dx, axis=3)
    total_s = term_one + term_two + term_three + term_four
    grad_step = along_x + decay_rate[None] * (total_s - step_size * along_x)
    grad_in = step_size[..., None] * raw_dx
    return grad_in, grad_step, grad_b, grad_c


def reference(inputs, step_size, decay_rate, b_proj, c_proj, grad_out, segment_ids):
    span_count = TOKENS // SPAN
    groups = inputs.shape[1]
    per_group = step_size.shape[2]

    def to_blocks(array_in):
        return array_in.reshape((span_count, SPAN) + array_in.shape[1:])

    def heads_of(block):
        return block.astype(jnp.float32).reshape(SPAN, groups, per_group, P_SIZE)

    def unpack(blocks):
        x_blk, dt_blk, b_blk, c_blk, dy_blk, seg_blk = blocks
        return heads_of(x_blk), dt_blk, b_blk.astype(jnp.float32), c_blk.astype(jnp.float32), heads_of(dy_blk), seg_blk

    pieces = (to_blocks(inputs), to_blocks(step_size), to_blocks(b_proj), to_blocks(c_proj), to_blocks(grad_out), to_blocks(segment_ids))

    def forward(carried, blocks):
        state_now, last_id = carried
        x_f, dt_f, b_f, c_f, dy_f, seg_f = unpack(blocks)
        decayed, forward_sum, reverse_sum = span_summary(x_f, dt_f, decay_rate, b_f, c_f, dy_f, seg_f)
        entering = state_now * (last_id == seg_f[0]).astype(jnp.float32)
        return (decayed[..., None, None] * entering + forward_sum, seg_f[-1]), entering

    zero_state = jnp.zeros((groups, per_group, P_SIZE, N), jnp.float32)
    start_id = jnp.array(-1, jnp.int32)
    final_fwd, states = lax.scan(forward, (zero_state, start_id), pieces)

    def backward(carried, blocks):
        adjoint_now, first_id = carried
        x_f, dt_f, b_f, c_f, dy_f, seg_f = unpack(blocks[:6])
        entering = blocks[6]
        decayed, forward_sum, reverse_sum = span_summary(x_f, dt_f, decay_rate, b_f, c_f, dy_f, seg_f)
        arriving = adjoint_now * (first_id == seg_f[-1]).astype(jnp.float32)
        gradients = span_grads(x_f, dt_f, decay_rate, b_f, c_f, dy_f, seg_f, entering, arriving)
        return (decayed[..., None, None] * arriving + reverse_sum, seg_f[0]), gradients

    final_bwd, gradients = lax.scan(backward, (zero_state, start_id), pieces + (states,), reverse=True)
    grad_in, grad_step, grad_b, grad_c = gradients
    return (grad_in.reshape(inputs.shape).astype(jnp.bfloat16), grad_step.reshape(step_size.shape), grad_b.reshape(b_proj.shape), grad_c.reshape(c_proj.shape))
```

```python
import functools

import jax
import jax.numpy as jnp
from jax import lax
from jax.experimental import pallas as pl
from jax.experimental.pallas import tpu as pltpu
from jax.sharding import Mesh, PartitionSpec as P

F32 = jnp.float32
BF16 = jnp.bfloat16
T = 256
G = 8
J = 4
W = 256
N = 128
ROWS = N + 8
DEC, FIRST, LAST, ELAST = N, N + 1, N + 2, N + 3
VMEM = pltpu.CompilerParams(vmem_limit_bytes=56 * 1024 * 1024)
Z, Y, C, X = "z", "y", "core", "head"


def dot(a, b):
    return lax.dot_general(a, b, (((1,), (0,)), ((), ())), preferred_element_type=F32)


def dot_t(a, b):
    return lax.dot_general(a, b, (((1,), (1,)), ((), ())), preferred_element_type=F32)


def split2(v):
    hi = v.astype(BF16)
    return hi, (v - hi.astype(F32)).astype(BF16)


def split3(v):
    hi = v.astype(BF16)
    rest = v - hi.astype(F32)
    mid = rest.astype(BF16)
    return hi, mid, (rest - mid.astype(F32)).astype(BF16)


def iota(shape, dim):
    return lax.broadcasted_iota(jnp.int32, shape, dim)


def head_ones():
    return (iota((8, W), 0) == iota((8, W), 1) // 64).astype(BF16)


def expander(g):
    k = iota((128, W), 0)
    return ((k < 96) & (k % 32 == J * g + iota((128, W), 1) // 64)).astype(BF16)


def head_sums(ones, z):
    hi, lo = split2(z)
    return dot_t(ones, hi) + dot_t(ones, lo)


def token_rows(seg_row):
    padded = jnp.concatenate([seg_row, jnp.zeros((7, T), F32)], axis=0).astype(BF16)
    ones = jnp.ones((8, T), BF16)
    return lax.dot_general(padded, ones, (((0,), (0,)), ((), ())), preferred_element_type=F32)


def masks(seg_row):
    seg_t = token_rows(seg_row)
    same = seg_t == seg_row
    low = same & (iota((T, T), 1) <= iota((T, T), 0))
    high = same & (iota((T, T), 1) >= iota((T, T), 0))
    first = seg_t[:, :N] == seg_t[0:1, :N]
    last = seg_t[:, :N] == seg_t[T - 1 : T, :N]
    return low, high, first, last


def order(i, pos):
    half = jnp.where(i < 4, 1 - pos[0], pos[0])
    return 4 * half + lax.rem(pos[1] + lax.rem(i, 4), 4)


def summary_kernel(
    pos, dt_ref, rate_ref, seg_ref, x_ref, dy_ref, b_ref, c_ref,
    xh_ref, xl_ref, dh_ref, dl_ref, bt_ref, ct_ref, qt_ref, fs_ref, fk_ref, rs_ref, rk_ref,
    x_s, dy_s, b_s, c_s, a_s, dt_s, et_s, first_s, last_s, meta_s,
):
    i = pl.program_id(0)
    g = order(i, pos)

    @pl.when(i == 0)
    def _():
        for j in range(J):
            for k in range(G):
                dt_s[J * k + j : J * k + j + 1, :] = dt_ref[k, j : j + 1, :]
                a_s[J * k + j : J * k + j + 1, :] = dt_ref[k, j : j + 1, :] * rate_ref[j, k]
        x_s[...] = jnp.swapaxes(x_ref[...], 0, 1)
        dy_s[...] = jnp.swapaxes(dy_ref[...], 0, 1)
        b_s[...] = jnp.swapaxes(b_ref[...], 0, 1)
        c_s[...] = jnp.swapaxes(c_ref[...], 0, 1)
        upto = (iota((T, T), 0) <= iota((T, T), 1)).astype(BF16)
        cum3 = dot(jnp.concatenate(split3(a_s[...]), axis=0), upto)
        cum = cum3[:32] + cum3[32:64] + cum3[64:96]
        e = jnp.exp(cum)
        q = jnp.exp(-cum) * dt_s[...]
        zero = jnp.zeros((32, T), F32)

        def columns(v):
            pieces = [piece.astype(F32) for piece in split3(v)]
            return jnp.transpose(jnp.concatenate(pieces + [zero], axis=0)).astype(BF16)

        et_s[...] = columns(e)
        qt_ref[...] = columns(q)
        seg_row = seg_ref[...].astype(F32)
        seg_t = token_rows(seg_row)
        first_s[...] = (seg_t[:, :N] == seg_t[0:1, :N]).astype(BF16)
        last_s[...] = (seg_t[:, :N] == seg_t[T - 1 : T, :N]).astype(BF16)
        meta_s[0:1, :] = seg_t[0:1, :]
        meta_s[1:2, :] = seg_t[T - 1 : T, :]

    spread = expander(g)
    e = dot(et_s[...], spread)
    q = dot(qt_ref[...], spread)
    xh, xl = split2(x_s[g].astype(F32) * q)
    dh, dl = split2(dy_s[g].astype(F32) * e)
    xh_ref[0], xl_ref[0], dh_ref[0], dl_ref[0] = xh, xl, dh, dl
    b, c = b_s[g], c_s[g]
    bt_ref[0], ct_ref[0] = b, c
    b_tr = jnp.transpose(b * last_s[...])
    c_tr = jnp.transpose(c * first_s[...])
    e_last = e[T - 1 : T, :]
    forward = (dot(b_tr, xh) + dot(b_tr, xl)) * e_last
    reverse = dot(c_tr, dh) + dot(c_tr, dl)
    first, last = meta_s[0:1, :], meta_s[1:2, :]
    whole = (first == last).astype(F32)
    tail = jnp.concatenate([e_last * whole, first, last, e_last, jnp.zeros((4, W), F32)], axis=0)

    def put(f_ref, r_ref):
        f_ref[0, :N, :] = forward
        f_ref[0, N:, :] = tail
        r_ref[0, :N, :] = reverse
        r_ref[0, N:, :] = tail

    pl.when(i < 4)(lambda: put(fs_ref, rs_ref))
    pl.when(i >= 4)(lambda: put(fk_ref, rk_ref))


def whole_spec(shape):
    return pl.BlockSpec(shape, lambda i, pos: (0,) * len(shape))


def summaries(pos, dt, rate, seg, x, dy, b, c):
    at = lambda i, pos: (order(i, pos), 0, 0)
    sent = pl.BlockSpec((1, ROWS, W), lambda i, pos: (jnp.minimum(i, 3), 0, 0))
    kept = pl.BlockSpec((1, ROWS, W), lambda i, pos: (jnp.maximum(i - 4, 0), 0, 0))
    wide = pl.BlockSpec((1, T, W), at)
    slim = pl.BlockSpec((1, T, N), at)
    grid = pltpu.PrefetchScalarGridSpec(
        num_scalar_prefetch=1,
        grid=(G,),
        in_specs=[
            whole_spec((G, J, T)),
            pl.BlockSpec(memory_space=pltpu.SMEM),
            whole_spec((1, T)),
            whole_spec((T, G, W)),
            whole_spec((T, G, W)),
            whole_spec((T, G, N)),
            whole_spec((T, G, N)),
        ],
        out_specs=[wide] * 4 + [slim] * 2 + [whole_spec((T, N))] + [sent, kept, sent, kept],
        scratch_shapes=[
            pltpu.VMEM((G, T, W), BF16),
            pltpu.VMEM((G, T, W), BF16),
            pltpu.VMEM((G, T, N), BF16),
            pltpu.VMEM((G, T, N), BF16),
            pltpu.VMEM((32, T), F32),
            pltpu.VMEM((32, T), F32),
            pltpu.VMEM((T, N), BF16),
            pltpu.VMEM((T, N), BF16),
            pltpu.VMEM((T, N), BF16),
            pltpu.VMEM((8, T), F32),
        ],
    )
    big = jax.ShapeDtypeStruct((G, T, W), BF16)
    thin = jax.ShapeDtypeStruct((G, T, N), BF16)
    block = jax.ShapeDtypeStruct((4, ROWS, W), F32)
    return pl.pallas_call(
        summary_kernel,
        grid_spec=grid,
        out_shape=[big] * 4 + [thin] * 2 + [jax.ShapeDtypeStruct((T, N), BF16)] + [block] * 4,
        compiler_params=VMEM,
        cost_estimate=pl.CostEstimate(flops=8 * 10**9, bytes_accessed=10 * 2**20, transcendentals=0),
        name="summaries",
    )(pos, dt, rate, seg, x, dy, b, c)


def local_kernel(
    seg_ref, xh_ref, xl_ref, dh_ref, dl_ref, b_ref, c_ref,
    gc_ref, gb_ref, raw_ref, u_ref,
    low_s, high_s,
):
    @pl.when(pl.program_id(0) == 0)
    def _():
        low, high, _, _ = masks(seg_ref[...].astype(F32))
        low_s[...] = low.astype(F32)
        high_s[...] = high.astype(F32)

    xh, xl, dh, dl = xh_ref[0], xl_ref[0], dh_ref[0], dl_ref[0]
    b, c = b_ref[0], c_ref[0]
    sums = dot_t(dh, xh) + dot_t(dh, xl) + dot_t(dl, xh)
    sh, sl = split2(sums * low_s[...])
    gc_ref[0] = dot(sh, b) + dot(sl, b)
    c_tr = jnp.transpose(c)
    gb_ref[0] = jnp.transpose(dot(c_tr, sh) + dot(c_tr, sl))
    wh, wl = split2(dot_t(c, b) * low_s[...])
    out = dot(wh, xh) + dot(wh, xl) + dot(wl, xh)
    u_ref[0] = head_sums(head_ones(), out * (dh.astype(F32) + dl.astype(F32)))
    vh, vl = split2(dot_t(b, c) * high_s[...])
    raw_ref[0] = dot(vh, dh) + dot(vh, dl) + dot(vl, dh)


def local_grads(seg, xh, xl, dh, dl, b, c):
    at = lambda i: (i, 0, 0)
    wide = pl.BlockSpec((1, T, W), at)
    slim = pl.BlockSpec((1, T, N), at)
    return pl.pallas_call(
        local_kernel,
        grid=(G,),
        in_specs=[pl.BlockSpec((1, T), lambda i: (0, 0))] + [wide] * 4 + [slim] * 2,
        out_specs=[slim, slim, wide, pl.BlockSpec((1, 8, T), at)],
        out_shape=[
            jax.ShapeDtypeStruct((G, T, N), F32),
            jax.ShapeDtypeStruct((G, T, N), F32),
            jax.ShapeDtypeStruct((G, T, W), F32),
            jax.ShapeDtypeStruct((G, 8, T), F32),
        ],
        scratch_shapes=[pltpu.VMEM((T, T), F32), pltpu.VMEM((T, T), F32)],
        compiler_params=VMEM,
        cost_estimate=pl.CostEstimate(flops=10 * 10**9, bytes_accessed=12 * 2**20, transcendentals=0),
        name="local_grads",
    )(seg, xh, xl, dh, dl, b, c)


def linked(earlier, later):
    return (earlier[LAST : LAST + 1, :] == later[FIRST : FIRST + 1, :]).astype(F32)


def join(earlier, later, out, rev):
    link = linked(earlier, later)
    near, far = (earlier, later) if rev else (later, earlier)
    out[:N, :] = near[:N, :] + (near[DEC : DEC + 1, :] * link) * far[:N, :]
    both = earlier[DEC : DEC + 1, :] * later[DEC : DEC + 1, :] * link
    out[N:, :] = jnp.concatenate(
        [both, earlier[FIRST : FIRST + 1, :], later[LAST : LAST + 1, :], jnp.zeros((5, W), F32)], axis=0
    )


def small_call(body, name, n_out, shape, pos, args, scratch=()):
    vmem = pl.BlockSpec(memory_space=pltpu.VMEM)
    return pl.pallas_call(
        body,
        in_specs=[pl.BlockSpec(memory_space=pltpu.SMEM)] + [vmem] * len(args),
        out_specs=[vmem] * n_out,
        out_shape=[jax.ShapeDtypeStruct(shape, F32)] * n_out,
        scratch_shapes=list(scratch),
        compiler_params=VMEM,
        cost_estimate=pl.CostEstimate(flops=10**9, bytes_accessed=2 * 2**20, transcendentals=0),
        name=name,
    )(pos, *args)


def chip_join(pos, kept, got, rev):
    def body(pos, kept, got, *outs):
        def go(earlier, later):
            for s in range(4):
                join(earlier.at[s], later.at[s], outs[s], rev)

        pl.when(pos[0] == 0)(lambda: go(kept, got))
        pl.when(pos[0] == 1)(lambda: go(got, kept))

    return small_call(body, "chip_join", 4, (ROWS, W), pos, (kept, got))


def plane_join(pos, blocks, rev):
    def body(pos, *refs):
        blocks, out, order_s, one, two = refs[:4], refs[4], refs[5], refs[6], refs[7]
        for s in range(4):
            order_s[lax.rem(pos[1] + 4 - s, 4)] = blocks[s][...]
        join(order_s.at[0], order_s.at[1], one, rev)
        join(order_s.at[2], order_s.at[3], two, rev)
        join(one, two, out, rev)

    scratch = [pltpu.VMEM((4, ROWS, W), F32), pltpu.VMEM((ROWS, W), F32), pltpu.VMEM((ROWS, W), F32)]
    return small_call(body, "plane_join", 1, (ROWS, W), pos, blocks, scratch)[0]


def plane_enter(pos, blocks, near, far, rev):
    def body(pos, *refs):
        blocks, near, far, outs, order_s, enter_s = refs[:4], refs[4], refs[5], refs[6:10], refs[10], refs[11]
        for s in range(4):
            order_s[lax.rem(pos[1] + 4 - s, 4)] = blocks[s][...]

        def link(one, two):
            return linked(two, one) if rev else linked(one, two)

        start, ahead = (3, -1) if rev else (0, 1)
        own = order_s.at[start]
        carry = near[:N, :] + (near[DEC : DEC + 1, :] * link(far, near)) * far[:N, :]
        enter_s[start] = link(near, own) * carry
        for step in range(3):
            here, there = start + step * ahead, start + (step + 1) * ahead
            block = order_s.at[here]
            hop = link(block, order_s.at[there])
            enter_s[there] = hop * (block[:N, :] + block[DEC : DEC + 1, :] * enter_s[here])
        for s in range(4):
            outs[s][...] = enter_s[lax.rem(pos[1] + s, 4)]

    scratch = [pltpu.VMEM((4, ROWS, W), F32), pltpu.VMEM((4, N, W), F32)]
    return small_call(body, "plane_enter", 4, (N, W), pos, (*blocks, near, far), scratch)


def device_enter(pos, entering, kept, got, rev):
    def body(pos, *refs):
        entering, kept, got, mine, other = refs[:4], refs[4], refs[5], refs[6], refs[7]

        def go(zero, one, direct, passed):
            inner = one if rev else zero
            for s in range(4):
                k, slot = lax.rem(pos[1] + 4 - s, 4), (4 - s) % 4
                link = linked(zero.at[slot], one.at[slot])
                block = inner.at[slot]
                direct[k] = entering[s][...]
                passed[k] = link * (block[:N, :] + block[DEC : DEC + 1, :] * entering[s][...])

        pl.when(pos[0] == 0)(lambda: go(kept, got, *((other, mine) if rev else (mine, other))))
        pl.when(pos[0] == 1)(lambda: go(got, kept, *((mine, other) if rev else (other, mine))))

    return small_call(body, "device_enter", 2, (4, N, W), pos, (*entering, kept, got))


def ring(count, shift):
    return [(i, (i + shift) % count) for i in range(count)]


def swap(v):
    return lax.ppermute(v, C, ring(2, 1))


def along_y(v, shift):
    return lax.ppermute(v, Y, ring(4, shift))


def along_z(v, shift):
    return lax.ppermute(v, Z, ring(8, shift))


def along_x(v, shift):
    return lax.ppermute(v, X, ring(4, shift))


def carried(pos, sent, kept, rev):
    sign = -1 if rev else 1
    got = swap(sent)
    blocks = chip_join(pos, kept, got, rev)
    blocks = [blocks[0]] + [along_y(blocks[s], s) for s in (1, 2, 3)]
    plane = plane_join(pos, blocks, rev)
    near, far = along_z(plane, sign), along_z(plane, 2 * sign)
    entering = plane_enter(pos, blocks, near, far, rev)
    entering = [entering[0]] + [along_y(entering[s], s) for s in (1, 2, 3)]
    mine, other = device_enter(pos, entering, kept, got, rev)
    return mine, swap(other)


def turned(i, pos):
    return lax.rem(2 * pos[2] + i, G)


def put_by_turn(i, outs, value):
    for s in range(4):

        @pl.when(i // 2 == s)
        def _(s=s):
            outs[s][0] = value


def state_kernel(
    pos, seg_ref, dh_ref, dl_ref, c_ref, gc_ref, u_ref, mine_ref, got_ref,
    o0, o1, o2, o3, u_out,
    first_s,
):
    i = pl.program_id(0)
    g = turned(i, pos)

    @pl.when(i == 0)
    def _():
        first_s[...] = masks(seg_ref[...].astype(F32))[2].astype(F32)

    state = jnp.where(g // 4 == pos[0], mine_ref[0], got_ref[0])
    sh, sl = split2(state)
    dh, dl = dh_ref[0], dl_ref[0]
    carried_c = dot_t(dh, sh) + dot_t(dh, sl) + dot_t(dl, sh)
    put_by_turn(i, (o0, o1, o2, o3), gc_ref[0] + first_s[...] * carried_c)
    c = c_ref[0] * first_s[...].astype(BF16)
    out = dot(c, sh) + dot(c, sl)
    u_out[0] = u_ref[0] + head_sums(head_ones(), out * (dh.astype(F32) + dl.astype(F32)))


def turn_specs():
    def spec(s):
        return pl.BlockSpec((1, T, N), lambda i, pos: (jnp.clip(i - 2 * s, 0, 1), 0, 0))

    return [spec(s) for s in range(4)]


def half_spec(rows):
    return pl.BlockSpec((1, rows, W), lambda i, pos: (lax.rem(turned(i, pos), 4), 0, 0))


def state_grads(pos, seg, dh, dl, c, gc, u, mine, got):
    at = lambda i, pos: (turned(i, pos), 0, 0)
    wide = pl.BlockSpec((1, T, W), at)
    slim = pl.BlockSpec((1, T, N), at)
    heads = pl.BlockSpec((1, 8, T), at)
    grid = pltpu.PrefetchScalarGridSpec(
        num_scalar_prefetch=1,
        grid=(G,),
        in_specs=[whole_spec((1, T)), wide, wide, slim, slim, heads, half_spec(N), half_spec(N)],
        out_specs=turn_specs() + [heads],
        scratch_shapes=[pltpu.VMEM((T, N), F32)],
    )
    return pl.pallas_call(
        state_kernel,
        grid_spec=grid,
        out_shape=[jax.ShapeDtypeStruct((2, T, N), F32)] * 4 + [jax.ShapeDtypeStruct((G, 8, T), F32)],
        compiler_params=VMEM,
        cost_estimate=pl.CostEstimate(flops=4 * 10**9, bytes_accessed=6 * 2**20, transcendentals=0),
        name="state_grads",
    )(pos, seg, dh, dl, c, gc, u, mine, got)


def adjoint_kernel(
    pos, seg_ref, dt_ref, rate_ref, qt_ref, xh_ref, xl_ref, b_ref, gb_ref, raw_ref, u_ref,
    smine_ref, sgot_ref, amine_ref, agot_ref, rk_ref, rs_ref,
    o0, o1, o2, o3, gi_ref, gs_ref,
    last_s, low_s, gi_s, v_s, u_s, k_s, dt_s, rate_s,
):
    i = pl.program_id(0)
    g = turned(i, pos)

    @pl.when(i == 0)
    def _():
        low, _, _, last = masks(seg_ref[...].astype(F32))
        last_s[...] = last.astype(F32)
        low_s[...] = low.astype(BF16)
        for j in range(J):
            for k in range(G):
                row = slice(J * k + j, J * k + j + 1)
                dt_s[row, :] = dt_ref[k, j : j + 1, :]
                rate_s[row, :] = jnp.full((1, T), rate_ref[j, k], F32)

    ours = g // 4 == pos[0]
    adjoint = jnp.where(ours, amine_ref[0], agot_ref[0])
    state = jnp.where(ours, smine_ref[0], sgot_ref[0])
    reverse = jnp.where(ours, rk_ref[0], rs_ref[0])
    ones = head_ones()
    crossing = state * (reverse[:N] + reverse[DEC : DEC + 1] * adjoint)
    k_s[g] = head_sums(ones, crossing)
    ah, al = split2(adjoint * reverse[ELAST : ELAST + 1])
    xh, xl = xh_ref[0], xl_ref[0]
    carried_b = dot_t(xh, ah) + dot_t(xh, al) + dot_t(xl, ah)
    put_by_turn(i, (o0, o1, o2, o3), gb_ref[0] + last_s[...] * carried_b)
    b = b_ref[0] * last_s[...].astype(BF16)
    raw = raw_ref[0] + dot(b, ah) + dot(b, al)
    q = dot(qt_ref[...], expander(g))
    gi_s[g] = (q * raw).astype(BF16)
    v_s[g] = head_sums(ones, raw * (xh.astype(F32) + xl.astype(F32)))
    u_s[g] = u_ref[0]

    @pl.when(i == G - 1)
    def _():
        gi_ref[...] = jnp.swapaxes(gi_s[...], 0, 1)
        v = jnp.concatenate([v_s[k][:J] for k in range(G)], axis=0)
        u = jnp.concatenate([u_s[k][:J] for k in range(G)], axis=0)
        cross = jnp.concatenate([k_s[k][:J] for k in range(G)], axis=0)
        total = jnp.sum(cross, axis=1, keepdims=True)
        change = v - u + jnp.where(iota((32, T), 1) == 0, total, 0.0)
        run3 = dot_t(jnp.concatenate(split3(change), axis=0), low_s[...])
        inter = run3[:32] + run3[32:64] + run3[64:96] + u
        grad = v / dt_s[...] + rate_s[...] * (inter - v)
        for k in range(G):
            gs_ref[k] = grad[J * k : J * k + J]


def adjoint_grads(pos, seg, dt, rate, qt, xh, xl, b, gb, raw, u, smine, sgot, amine, agot, rk, rs):
    at = lambda i, pos: (turned(i, pos), 0, 0)
    wide = pl.BlockSpec((1, T, W), at)
    slim = pl.BlockSpec((1, T, N), at)
    heads = pl.BlockSpec((1, 8, T), at)
    slot = pl.BlockSpec((1, ROWS, W), lambda i, pos: (lax.rem(turned(i, pos) + 4 - pos[1], 4), 0, 0))
    grid = pltpu.PrefetchScalarGridSpec(
        num_scalar_prefetch=1,
        grid=(G,),
        in_specs=[
            whole_spec((1, T)),
            whole_spec((G, J, T)),
            pl.BlockSpec(memory_space=pltpu.SMEM),
            whole_spec((T, N)),
            wide, wide, slim, slim, wide, heads,
            half_spec(N), half_spec(N), half_spec(N), half_spec(N), slot, slot,
        ],
        out_specs=turn_specs() + [whole_spec((T, G, W)), whole_spec((G, J, T))],
        scratch_shapes=[
            pltpu.VMEM((T, N), F32),
            pltpu.VMEM((T, T), BF16),
            pltpu.VMEM((G, T, W), BF16),
            pltpu.VMEM((G, 8, T), F32),
            pltpu.VMEM((G, 8, T), F32),
            pltpu.VMEM((G, 8, N), F32),
            pltpu.VMEM((32, T), F32),
            pltpu.VMEM((32, T), F32),
        ],
    )
    return pl.pallas_call(
        adjoint_kernel,
        grid_spec=grid,
        out_shape=[jax.ShapeDtypeStruct((2, T, N), F32)] * 4
        + [jax.ShapeDtypeStruct((T, G, W), BF16), jax.ShapeDtypeStruct((G, J, T), F32)],
        compiler_params=VMEM,
        cost_estimate=pl.CostEstimate(flops=6 * 10**9, bytes_accessed=9 * 2**20, transcendentals=0),
        name="adjoint_grads",
    )(pos, seg, dt, rate, qt, xh, xl, b, gb, raw, u, smine, sgot, amine, agot, rk, rs)


def over_heads(parts):
    got = [along_x(parts[s], s) for s in (1, 2, 3)]
    return jnp.transpose(parts[0] + got[0] + got[1] + got[2], (1, 0, 2))


def per_device(inputs, step_size, decay_rate, b_proj, c_proj, grad_out, segment_ids):
    pos = jnp.stack([lax.axis_index(C), lax.axis_index(Y), lax.axis_index(X)]).astype(jnp.int32)
    seg = segment_ids.reshape(1, T)
    dt = jnp.transpose(step_size, (1, 2, 0))
    rate = jnp.transpose(decay_rate)
    xh, xl, dh, dl, b, c, qt, fs, fk, rs, rk = summaries(pos, dt, rate, seg, inputs, grad_out, b_proj, c_proj)
    gc, gb, raw, u = local_grads(seg, xh, xl, dh, dl, b, c)
    smine, sgot = carried(pos, fs, fk, False)
    amine, agot = carried(pos, rs, rk, True)
    *parts_c, u = state_grads(pos, seg, dh, dl, c, gc, u, smine, sgot)
    total_c = over_heads(parts_c)
    *parts_b, grad_in, grad_step = adjoint_grads(
        pos, seg, dt, rate, qt, xh, xl, b, gb, raw, u, smine, sgot, amine, agot, rk, rs
    )
    total_b = over_heads(parts_b)
    return grad_in, jnp.transpose(grad_step, (2, 0, 1)), total_b, total_c


def solution(mesh):
    fine = Mesh(mesh.devices.reshape(8, 4, 2, 4), (Z, Y, C, X))
    ctx = (Z, Y, C)
    placed = (
        P(ctx, None, X),
        P(ctx, None, X),
        P(None, X),
        P(ctx, None, None),
        P(ctx, None, None),
        P(ctx, None, X),
        P(ctx),
    )
    return jax.shard_map(
        per_device,
        mesh=fine,
        in_specs=placed,
        out_specs=(P(ctx, None, X), P(ctx, None, X), P(ctx, X, None), P(ctx, X, None)),
        check_vma=False,
    )
```

```python
import functools

import jax
import jax.numpy as jnp
from jax import lax
from jax.experimental import pallas as pl
from jax.experimental.pallas import tpu as pltpu
from jax.sharding import Mesh, PartitionSpec as P

F32 = jnp.float32
BF16 = jnp.bfloat16
T = 256
G = 8
J = 4
W = 256
N = 128
ROWS = N + 8
DEC, FIRST, LAST, ELAST = N, N + 1, N + 2, N + 3
HBM = pl.BlockSpec(memory_space=pltpu.HBM)
VMEM = pl.BlockSpec(memory_space=pltpu.VMEM)
SMEM = pl.BlockSpec(memory_space=pltpu.SMEM)
Z, Y, C, X = "z", "y", "core", "head"


def dot(a, b):
    return lax.dot_general(a, b, (((1,), (0,)), ((), ())), preferred_element_type=F32)


def dot_t(a, b):
    return lax.dot_general(a, b, (((1,), (1,)), ((), ())), preferred_element_type=F32)


def split2(v):
    hi = v.astype(BF16)
    return hi, (v - hi.astype(F32)).astype(BF16)


def split3(v):
    hi = v.astype(BF16)
    rest = v - hi.astype(F32)
    mid = rest.astype(BF16)
    return hi, mid, (rest - mid.astype(F32)).astype(BF16)


def iota(shape, dim):
    return lax.broadcasted_iota(jnp.int32, shape, dim)


def head_ones():
    return (iota((8, W), 0) == iota((8, W), 1) // 64).astype(BF16)


def expander(g):
    k = iota((128, W), 0)
    return ((k < 96) & (k % 32 == J * g + iota((128, W), 1) // 64)).astype(BF16)


def head_sums(ones, z):
    hi, lo = split2(z)
    return dot_t(ones, hi) + dot_t(ones, lo)


def token_rows(seg_row):
    padded = jnp.concatenate([seg_row, jnp.zeros((7, T), F32)], axis=0).astype(BF16)
    ones = jnp.ones((8, T), BF16)
    return lax.dot_general(padded, ones, (((0,), (0,)), ((), ())), preferred_element_type=F32)


def lows(seg_t, seg_row):
    return (seg_t == seg_row) & (iota((T, T), 1) <= iota((T, T), 0))


def highs(seg_t, seg_row):
    return (seg_t == seg_row) & (iota((T, T), 1) >= iota((T, T), 0))


def firsts(seg_t):
    return seg_t[:, :N] == seg_t[0:1, :N]


def lasts(seg_t):
    return seg_t[:, :N] == seg_t[T - 1 : T, :N]


def place():
    return lax.axis_index(C), lax.axis_index(Y), lax.axis_index(X)


def copy(source, target, sem):
    return pltpu.make_async_copy(source, target, sem)


def start(*copies):
    for one in copies:
        one.start()


def wait(*copies):
    for one in copies:
        one.wait()


def sds(*shape, dtype=F32):
    return jax.ShapeDtypeStruct(shape, dtype)


def call(kernel, args, specs, outs, scratch, name, mega, mib, out_spec=HBM, **more):
    return pl.pallas_call(
        kernel,
        in_specs=specs,
        out_specs=[out_spec] * len(outs),
        out_shape=outs,
        scratch_shapes=scratch,
        compiler_params=pltpu.CompilerParams(vmem_limit_bytes=mib * 2**20),
        cost_estimate=pl.CostEstimate(flops=mega * 10**3, bytes_accessed=2**10, transcendentals=0),
        name=name,
        **more,
    )(*args)


def columns(v):
    pieces = [piece.astype(F32) for piece in split3(v)] + [jnp.zeros((32, T), F32)]
    return jnp.transpose(jnp.concatenate(pieces, axis=0)).astype(BF16)


def summary_kernel(
    rate_hbm, dt_hbm, seg_hbm, x_hbm, dy_hbm, b_hbm, c_hbm,
    xh_hbm, xl_hbm, dh_hbm, dl_hbm, bt_hbm, ct_hbm, qt_hbm, fs_hbm, fk_hbm, rs_hbm, rk_hbm,
    rate, dt_v, seg_v, x_v, dy_v, b_v, c_v, bt_s, ct_s, xh_s, xl_s, dh_s, dl_s, f_s, r_s,
    a_s, dt_s, et_s, qt_s, in_sem, bc_sem, xd_sem, st_sem,
):
    core, y, _ = place()
    loads = [
        copy(source, target, in_sem.at[k])
        for k, (source, target) in enumerate(
            [
                (rate_hbm, rate), (dt_hbm, dt_v), (seg_hbm, seg_v),
                (b_hbm, b_v), (x_hbm, x_v), (c_hbm, c_v), (dy_hbm, dy_v),
            ]
        )
    ]
    start(*loads)
    wait(*loads[:3])
    for j in range(J):
        for k in range(G):
            row = slice(J * k + j, J * k + j + 1)
            dt_s[row, :] = dt_v[k, j : j + 1, :]
            a_s[row, :] = dt_v[k, j : j + 1, :] * rate[j, k]
    upto = (iota((T, T), 0) <= iota((T, T), 1)).astype(BF16)
    cum3 = dot(jnp.concatenate(split3(a_s[...]), axis=0), upto)
    cum = cum3[:32] + cum3[32:64] + cum3[64:96]
    et_s[...] = columns(jnp.exp(cum))
    qt_s[...] = columns(jnp.exp(-cum) * dt_s[...])
    seg_t = token_rows(seg_v[...].astype(F32))
    first_mask, last_mask = firsts(seg_t).astype(BF16), lasts(seg_t).astype(BF16)
    first, last = seg_t[0:1, :], seg_t[T - 1 : T, :]
    whole = (first == last).astype(F32)
    outs = [copy(qt_s, qt_hbm, bc_sem.at[2])]

    def order(i):
        return 4 * (1 - core if i < 4 else core) + lax.rem(y + i % 4, 4)

    def side(load_w, load_v, w_v, v_v, wt_s, wt_hbm, k, col, mask, hi_s, lo_s, hi_hbm, lo_hbm, out_s, sent, kept):
        load_w.wait()
        wt_s[...] = jnp.swapaxes(w_v[...], 0, 1)
        outs.append(copy(wt_s, wt_hbm, bc_sem.at[k]))
        outs[-1].start()
        load_v.wait()
        hi_s[...] = jnp.swapaxes(v_v[...], 0, 1)
        for i in range(G):
            g = order(i)
            spread = expander(g)
            scale = dot(col[...], spread)
            e_last = dot(et_s[T - 16 :, :], spread)[15:16]
            hi, lo = split2(hi_s[g].astype(F32) * scale)
            hi_s[g], lo_s[g] = hi, lo
            w = jnp.transpose(wt_s[g] * mask)
            block = dot(w, hi) + dot(w, lo)
            out_s[i, :N, :] = block if k else block * e_last
            out_s[i, N:, :] = jnp.concatenate(
                [e_last * whole, first, last, e_last, jnp.zeros((4, W), F32)], axis=0
            )
            started = copy(out_s.at[i], (sent if i < 4 else kept).at[i % 4], st_sem.at[8 * k + i])
            started.start()
            outs.append(started)
        outs.append(copy(hi_s, hi_hbm, xd_sem.at[2 * k]))
        outs.append(copy(lo_s, lo_hbm, xd_sem.at[2 * k + 1]))
        start(*outs[-2:])

    outs[0].start()
    side(
        loads[3], loads[4], b_v, x_v, bt_s, bt_hbm, 0, qt_s, last_mask,
        xh_s, xl_s, xh_hbm, xl_hbm, f_s, fs_hbm, fk_hbm,
    )
    side(
        loads[5], loads[6], c_v, dy_v, ct_s, ct_hbm, 1, et_s, first_mask,
        dh_s, dl_s, dh_hbm, dl_hbm, r_s, rs_hbm, rk_hbm,
    )
    wait(*outs)


def summaries(dt, rate, seg, x, dy, b, c):
    big, thin, block = sds(G, T, W, dtype=BF16), sds(G, T, N, dtype=BF16), sds(4, ROWS, W)
    tall = pltpu.VMEM((G, T, W), BF16)
    return call(
        summary_kernel,
        (rate, dt, seg, x, dy, b, c),
        [HBM] * 7,
        [big] * 4 + [thin] * 2 + [sds(T, N, dtype=BF16)] + [block] * 4,
        [
            pltpu.SMEM((J, G), F32), pltpu.VMEM((G, J, T), F32), pltpu.VMEM((1, T), jnp.int32),
            pltpu.VMEM((T, G, W), BF16), pltpu.VMEM((T, G, W), BF16),
            pltpu.VMEM((T, G, N), BF16), pltpu.VMEM((T, G, N), BF16),
            pltpu.VMEM((G, T, N), BF16), pltpu.VMEM((G, T, N), BF16),
            tall, tall, tall, tall,
            pltpu.VMEM((G, ROWS, W), F32), pltpu.VMEM((G, ROWS, W), F32),
            pltpu.VMEM((32, T), F32), pltpu.VMEM((32, T), F32),
            pltpu.VMEM((T, N), BF16), pltpu.VMEM((T, N), BF16),
            pltpu.SemaphoreType.DMA((7,)), pltpu.SemaphoreType.DMA((3,)),
            pltpu.SemaphoreType.DMA((4,)), pltpu.SemaphoreType.DMA((16,)),
        ],
        "summaries",
        8000,
        60,
    )


def local_kernel(g0, count, seg_ref, *refs):
    ins, outs = refs[:6], refs[-4:]
    seg_row = seg_ref[...].astype(F32)
    seg_t = token_rows(seg_row)
    low, high = lows(seg_t, seg_row).astype(F32), highs(seg_t, seg_row).astype(F32)
    ones = head_ones()
    for i in range(count):
        xh, xl, dh, dl, b, c = [ref[g0 + i] for ref in ins]
        sums = dot_t(dh, xh) + dot_t(dh, xl) + dot_t(dl, xh)
        sh, sl = split2(sums * low)
        outs[0][i] = dot(sh, b) + dot(sl, b)
        c_tr = jnp.transpose(c)
        outs[1][i] = jnp.transpose(dot(c_tr, sh) + dot(c_tr, sl))
        wh, wl = split2(dot_t(c, b) * low)
        out = dot(wh, xh) + dot(wh, xl) + dot(wl, xh)
        outs[3][i] = head_sums(ones, out * (dh.astype(F32) + dl.astype(F32)))
        vh, vl = split2(dot_t(b, c) * high)
        outs[2][i] = dot(vh, dh) + dot(vh, dl) + dot(vl, dh)


def local_grads(g0, count, seg, data, after):
    return call(
        functools.partial(local_kernel, g0, count),
        (seg, *data, *after),
        [VMEM] * 7 + [HBM] * len(after),
        [sds(count, T, N), sds(count, T, N), sds(count, T, W), sds(count, 8, T)],
        [],
        "local_grads",
        3000,
        12,
        VMEM,
    )


def piece(parts, g):
    for part in parts:
        if g < part.shape[0]:
            return part.at[g]
        g -= part.shape[0]


def linked(earlier, later):
    return (earlier[LAST : LAST + 1, :] == later[FIRST : FIRST + 1, :]).astype(F32)


def join(earlier, later, out, rev):
    link = linked(earlier, later)
    near, far = (earlier, later) if rev else (later, earlier)
    out[:N, :] = near[:N, :] + (near[DEC : DEC + 1, :] * link) * far[:N, :]
    both = earlier[DEC : DEC + 1, :] * later[DEC : DEC + 1, :] * link
    out[N:, :] = jnp.concatenate(
        [both, earlier[FIRST : FIRST + 1, :], later[LAST : LAST + 1, :], jnp.zeros((5, W), F32)], axis=0
    )


def load_all(pairs, sems):
    loads = [copy(source, target, sems.at[k]) for k, (source, target) in enumerate(pairs)]
    start(*loads)
    return loads


def block(*lead):
    return pltpu.VMEM((*lead, ROWS, W), F32)


def sems(count):
    return pltpu.SemaphoreType.DMA((count,))


def small_call(body, args, after, outs, scratch, name):
    def kernel(*refs):
        body(*refs[: len(args)], *refs[len(args) + len(after) :])

    specs = [VMEM] * len(args) + [HBM] * len(after)
    return call(kernel, (*args, *after), specs, outs, scratch, name, 1000, 8, VMEM)


def chip_join(kept, got, rev, after=()):
    def body(kept, got, *outs):
        def go(earlier, later):
            for s in range(4):
                join(earlier.at[s], later.at[s], outs[s], rev)

        pl.when(place()[0] == 0)(lambda: go(kept, got))
        pl.when(place()[0] == 1)(lambda: go(got, kept))

    return small_call(body, (kept, got), after, [sds(ROWS, W)] * 4, [], "chip_join")


def by_y(blocks, go):
    y = place()[1]
    for k in range(4):
        pl.when(y == k)(lambda k=k: go([blocks[(k - there) % 4] for there in range(4)], k))


def plane_join(blocks, rev, after=()):
    def body(*refs):
        blocks, out, one, two = refs[:4], refs[4], refs[5], refs[6]

        def go(order, _):
            join(order[0], order[1], one, rev)
            join(order[2], order[3], two, rev)
            join(one, two, out, rev)

        by_y(blocks, go)

    return small_call(body, blocks, after, [sds(ROWS, W)], [block(), block()], "plane_join")[0]


def plane_enter(blocks, near, far, rev, after=()):
    def body(*refs):
        blocks, near, far, outs = refs[:4], refs[4], refs[5], refs[6:]

        def link(one, two):
            return linked(two, one) if rev else linked(one, two)

        def go(order, y):
            first, ahead = (3, -1) if rev else (0, 1)
            carry = near[:N, :] + (near[DEC : DEC + 1, :] * link(far, near)) * far[:N, :]
            carry = link(near, order[first]) * carry
            for step in range(4):
                here = first + step * ahead
                outs[(here - y) % 4][...] = carry
                if step < 3:
                    one = order[here]
                    carry = link(one, order[here + ahead]) * (one[:N, :] + one[DEC : DEC + 1, :] * carry)

        by_y(blocks, go)

    return small_call(body, (*blocks, near, far), after, [sds(N, W)] * 4, [], "plane_enter")


def device_enter(entering, kept, got, rev, after=()):
    inner = 1 if rev else 0

    def body(*refs):
        entering, kept, got, mine, other = refs[:4], refs[4], refs[5], refs[6], refs[7]
        core, y, _ = place()

        def go(near, far, direct, passed):
            for s in range(4):
                k, slot = lax.rem(y + 4 - s, 4), (4 - s) % 4
                one, two = near.at[slot], far.at[slot]
                link = linked(two, one) if rev else linked(one, two)
                direct[k] = entering[s][...]
                passed[k] = link * (one[:N, :] + one[DEC : DEC + 1, :] * entering[s][...])

        pl.when(core == inner)(lambda: go(kept, got, mine, other))
        pl.when(core != inner)(lambda: go(got, kept, other, mine))

    args = (*entering, kept, got)
    return small_call(body, args, after, [sds(4, N, W)] * 2, [], "device_enter")


def ring(count, shift):
    return [(i, (i + shift) % count) for i in range(count)]


def swap(v):
    return lax.ppermute(v, C, ring(2, 1))


def along_y(v, shift):
    return lax.ppermute(v, Y, ring(4, shift))


def along_z(v, shift):
    return lax.ppermute(v, Z, ring(8, shift))


def along_x(v, shift):
    return lax.ppermute(v, X, ring(4, shift))


def of_half(core, g, mine, got):
    return jnp.where(core == g // 4, mine[g % 4], got[g % 4])


def reverse_block(core, y, g, kept, sent, rows):
    slot = lax.rem(g % 4 + 4 - y, 4)
    return jnp.where(core == g // 4, kept[slot, rows, :], sent[slot, rows, :])


def sum_kernel(rev, n_parts, seg_ref, hi_ref, lo_ref, mine, got, *refs):
    if rev:
        kept, sent, refs = refs[0], refs[1], refs[2:]
    parts, outs = refs[:n_parts], refs[-4:]
    core, y, x = place()
    seg_t = token_rows(seg_ref[...].astype(F32))
    mask = (lasts(seg_t) if rev else firsts(seg_t)).astype(F32)
    for g in range(G):
        state = of_half(core, g, mine, got)
        if rev:
            state = state * reverse_block(core, y, g, kept, sent, slice(N, ROWS))[ELAST - N : ELAST - N + 1]
        sh, sl = split2(state)
        hi, lo = hi_ref[g], lo_ref[g]
        whole = piece(parts, g)[...] + mask * (dot_t(hi, sh) + dot_t(hi, sl) + dot_t(lo, sh))
        shift = lax.rem(g // 2 + 4 - x, 4)
        for s in range(4):

            @pl.when(shift == s)
            def _(s=s, whole=whole):
                outs[s][g % 2] = whole


def summed(rev, seg, hi, lo, mine, got, more, parts, after):
    args = (seg, hi, lo, mine, got, *more, *parts, *after)
    return call(
        functools.partial(sum_kernel, rev, len(parts)),
        args,
        [VMEM] * (len(args) - len(after)) + [HBM] * len(after),
        [sds(2, T, N)] * 4,
        [],
        "summed",
        3000,
        12,
        VMEM,
    )


def token_kernel(
    n_parts, rate, seg_ref, dt_ref, qt_ref, xh_ref, xl_ref, dh_ref, dl_ref, b_ref, c_ref,
    smine, sgot, amine, agot, kept, sent, *refs,
):
    raws, us = refs[:n_parts], refs[n_parts : 2 * n_parts]
    gi_ref, gs_ref, gi_s, v_s, u_s, k_s, dt_s, rate_s = refs[-8:]
    core, y, _ = place()
    for j in range(J):
        for k in range(G):
            row = slice(J * k + j, J * k + j + 1)
            dt_s[row, :] = dt_ref[k, j : j + 1, :]
            rate_s[row, :] = jnp.full((1, T), rate[j, k], F32)
    seg_row = seg_ref[...].astype(F32)
    seg_t = token_rows(seg_row)
    first, last = firsts(seg_t).astype(BF16), lasts(seg_t).astype(BF16)
    ones = head_ones()
    for g in range(G):
        state, adjoint = of_half(core, g, smine, sgot), of_half(core, g, amine, agot)
        reverse = reverse_block(core, y, g, kept, sent, slice(0, ROWS))
        crossing = state * (reverse[:N] + reverse[DEC : DEC + 1] * adjoint)
        k_s[g] = head_sums(ones, crossing)
        sh, sl = split2(state)
        c = c_ref[g] * first
        out = dot(c, sh) + dot(c, sl)
        u_s[g] = piece(us, g)[...] + head_sums(ones, out * (dh_ref[g].astype(F32) + dl_ref[g].astype(F32)))
        ah, al = split2(adjoint * reverse[ELAST : ELAST + 1])
        b = b_ref[g] * last
        raw = piece(raws, g)[...] + dot(b, ah) + dot(b, al)
        q = dot(qt_ref[...], expander(g))
        gi_s[g] = (q * raw).astype(BF16)
        v_s[g] = head_sums(ones, raw * (xh_ref[g].astype(F32) + xl_ref[g].astype(F32)))
    gi_ref[...] = jnp.swapaxes(gi_s[...], 0, 1)
    v = jnp.concatenate([v_s[k][:J] for k in range(G)], axis=0)
    u = jnp.concatenate([u_s[k][:J] for k in range(G)], axis=0)
    cross = jnp.concatenate([k_s[k][:J] for k in range(G)], axis=0)
    total = jnp.sum(cross, axis=1, keepdims=True)
    change = v - u + jnp.where(iota((32, T), 1) == 0, total, 0.0)
    run3 = dot_t(jnp.concatenate(split3(change), axis=0), lows(seg_t, seg_row).astype(BF16))
    inter = run3[:32] + run3[32:64] + run3[64:96] + u
    grad = v / dt_s[...] + rate_s[...] * (inter - v)
    for k in range(G):
        gs_ref[k] = grad[J * k : J * k + J]


def token_grads(args, raws, us, after):
    args = (*args, *raws, *us, *after)
    heads = pltpu.VMEM((G, 8, T), F32)
    return call(
        functools.partial(token_kernel, len(raws)),
        args,
        [SMEM] + [VMEM] * (len(args) - 1 - len(after)) + [HBM] * len(after),
        [sds(T, G, W, dtype=BF16), sds(G, J, T)],
        [
            pltpu.VMEM((G, T, W), BF16), heads, heads, pltpu.VMEM((G, 8, N), F32),
            pltpu.VMEM((32, T), F32), pltpu.VMEM((32, T), F32),
        ],
        "token_grads", 6000, 16, VMEM,
    )


def over_heads(parts):
    return [along_x(parts[s], s) for s in (1, 2, 3)]


def total(own, got):
    return jnp.transpose(own + got[0] + got[1] + got[2], (1, 0, 2))


def per_device(inputs, step_size, decay_rate, b_proj, c_proj, grad_out, segment_ids):
    seg = segment_ids.reshape(1, T)
    dt = jnp.transpose(step_size, (1, 2, 0))
    rate = jnp.transpose(decay_rate)
    xh, xl, dh, dl, b, c, qt, fs, fk, rs, rk = summaries(dt, rate, seg, inputs, grad_out, b_proj, c_proj)
    data = (xh, xl, dh, dl, b, c)

    def spread_y(blocks):
        return [blocks[0]] + [along_y(blocks[s], s) for s in (1, 2, 3)]

    def local(g0, count, *after):
        return local_grads(g0, count, seg, data, after)

    fgot, rgot = swap(fs), swap(rs)
    fjoined = chip_join(fk, fgot, 0)
    rjoined = chip_join(rk, rgot, 1, (fjoined[0],))
    held = [local(0, 3, rjoined[0])]
    fblocks, rblocks = spread_y(fjoined), spread_y(rjoined)
    fplane = plane_join(fblocks, 0, (held[0][3],))
    held.append(local(3, 2, fplane))
    rplane = plane_join(rblocks, 1, (held[1][3],))
    held.append(local(5, 3, rplane))
    fenter = plane_enter(fblocks, along_z(fplane, 1), along_z(fplane, 2), 0, (held[2][3],))
    renter = plane_enter(rblocks, along_z(rplane, -1), along_z(rplane, -2), 1, (fenter[0],))
    gc, gb, raw, u = zip(*held)
    smine, fother = device_enter(spread_y(fenter), fk, fgot, 0)
    sgot = swap(fother)
    parts_c = summed(False, seg, dh, dl, smine, sgot, (), gc, ())
    got_c = over_heads(parts_c)
    amine, rother = device_enter(spread_y(renter), rk, rgot, 1, (smine,))
    agot = swap(rother)
    parts_b = summed(True, seg, xh, xl, amine, agot, (rk, rs), gb, (parts_c[0],))
    got_b = over_heads(parts_b)
    grad_in, grad_step = token_grads(
        (rate, seg, dt, qt, xh, xl, dh, dl, b, c, smine, sgot, amine, agot, rk, rs), raw, u, (parts_b[0],)
    )
    total_c, total_b = total(parts_c[0], got_c), total(parts_b[0], got_b)
    return grad_in, jnp.transpose(grad_step, (2, 0, 1)), total_b, total_c


def solution(mesh):
    fine = Mesh(mesh.devices.reshape(8, 4, 2, 4), (Z, Y, C, X))
    ctx = (Z, Y, C)
    placed = (
        P(ctx, None, X),
        P(ctx, None, X),
        P(None, X),
        P(ctx, None, None),
        P(ctx, None, None),
        P(ctx, None, X),
        P(ctx),
    )
    return jax.shard_map(
        per_device,
        mesh=fine,
        in_specs=placed,
        out_specs=(P(ctx, None, X), P(ctx, None, X), P(ctx, X, None), P(ctx, X, None)),
        check_vma=False,
    )
```

```python
import functools

import jax
import jax.numpy as jnp
from jax import lax
from jax.experimental import pallas as pl
from jax.experimental.pallas import tpu as pltpu
from jax.sharding import Mesh, PartitionSpec as P

F32 = jnp.float32
BF16 = jnp.bfloat16
T = 256
G = 8
J = 4
W = 256
N = 128
ROWS = N + 8
DEC, FIRST, LAST, ELAST = N, N + 1, N + 2, N + 3
HBM = pl.BlockSpec(memory_space=pltpu.HBM)
VMEM = pl.BlockSpec(memory_space=pltpu.VMEM)
SMEM = pl.BlockSpec(memory_space=pltpu.SMEM)
Z, Y, C, X = "z", "y", "core", "head"


def dot(a, b):
    return lax.dot_general(a, b, (((1,), (0,)), ((), ())), preferred_element_type=F32)


def dot_t(a, b):
    return lax.dot_general(a, b, (((1,), (1,)), ((), ())), preferred_element_type=F32)


def split2(v):
    hi = v.astype(BF16)
    return hi, (v - hi.astype(F32)).astype(BF16)


def split3(v):
    hi = v.astype(BF16)
    rest = v - hi.astype(F32)
    mid = rest.astype(BF16)
    return hi, mid, (rest - mid.astype(F32)).astype(BF16)


def iota(shape, dim):
    return lax.broadcasted_iota(jnp.int32, shape, dim)


def head_ones():
    return (iota((8, W), 0) == iota((8, W), 1) // 64).astype(BF16)


def expander(g):
    k = iota((128, W), 0)
    return ((k < 96) & (k % 32 == J * g + iota((128, W), 1) // 64)).astype(BF16)


def head_sums(ones, z):
    hi, lo = split2(z)
    return dot_t(ones, hi) + dot_t(ones, lo)


def token_rows(seg_row):
    padded = jnp.concatenate([seg_row, jnp.zeros((7, T), F32)], axis=0).astype(BF16)
    ones = jnp.ones((8, T), BF16)
    return lax.dot_general(padded, ones, (((0,), (0,)), ((), ())), preferred_element_type=F32)


def lows(seg_t, seg_row):
    return (seg_t == seg_row) & (iota((T, T), 1) <= iota((T, T), 0))


def highs(seg_t, seg_row):
    return (seg_t == seg_row) & (iota((T, T), 1) >= iota((T, T), 0))


def firsts(seg_t):
    return seg_t[:, :N] == seg_t[0:1, :N]


def lasts(seg_t):
    return seg_t[:, :N] == seg_t[T - 1 : T, :N]


def place():
    return lax.axis_index(C), lax.axis_index(Y), lax.axis_index(X)


def copy(source, target, sem):
    return pltpu.make_async_copy(source, target, sem)


def start(*copies):
    for one in copies:
        one.start()


def wait(*copies):
    for one in copies:
        one.wait()


def sds(*shape, dtype=F32):
    return jax.ShapeDtypeStruct(shape, dtype)


def call(kernel, args, specs, outs, scratch, name, mega, mib, out_spec=HBM, **more):
    return pl.pallas_call(
        kernel,
        in_specs=specs,
        out_specs=[out_spec] * len(outs),
        out_shape=outs,
        scratch_shapes=scratch,
        compiler_params=pltpu.CompilerParams(vmem_limit_bytes=mib * 2**20),
        cost_estimate=pl.CostEstimate(flops=mega * 10**3, bytes_accessed=2**10, transcendentals=0),
        name=name,
        **more,
    )(*args)


def columns(v):
    pieces = [piece.astype(F32) for piece in split3(v)] + [jnp.zeros((32, T), F32)]
    return jnp.transpose(jnp.concatenate(pieces, axis=0)).astype(BF16)


def summary_kernel(
    rate_hbm, dt_hbm, seg_hbm, x_hbm, dy_hbm, b_hbm, c_hbm,
    xh_hbm, xl_hbm, dh_hbm, dl_hbm, bt_hbm, ct_hbm, qt_hbm, fs_hbm, fk_hbm, rs_hbm, rk_hbm,
    rate, dt_v, seg_v, x_v, dy_v, b_v, c_v, bt_s, ct_s, xh_s, xl_s, dh_s, dl_s, f_s, r_s,
    a_s, dt_s, et_s, qt_s, in_sem, bc_sem, xd_sem, st_sem,
):
    core, y, _ = place()
    loads = [
        copy(source, target, in_sem.at[k])
        for k, (source, target) in enumerate(
            [
                (rate_hbm, rate), (dt_hbm, dt_v), (seg_hbm, seg_v),
                (b_hbm, b_v), (x_hbm, x_v), (c_hbm, c_v), (dy_hbm, dy_v),
            ]
        )
    ]
    start(*loads)
    wait(*loads[:3])
    for j in range(J):
        for k in range(G):
            row = slice(J * k + j, J * k + j + 1)
            dt_s[row, :] = dt_v[k, j : j + 1, :]
            a_s[row, :] = dt_v[k, j : j + 1, :] * rate[j, k]
    upto = (iota((T, T), 0) <= iota((T, T), 1)).astype(BF16)
    cum3 = dot(jnp.concatenate(split3(a_s[...]), axis=0), upto)
    cum = cum3[:32] + cum3[32:64] + cum3[64:96]
    et_s[...] = columns(jnp.exp(cum))
    qt_s[...] = columns(jnp.exp(-cum) * dt_s[...])
    seg_t = token_rows(seg_v[...].astype(F32))
    first_mask, last_mask = firsts(seg_t).astype(BF16), lasts(seg_t).astype(BF16)
    first, last = seg_t[0:1, :], seg_t[T - 1 : T, :]
    whole = (first == last).astype(F32)
    outs = [copy(qt_s, qt_hbm, bc_sem.at[2])]

    def order(i):
        return 4 * (1 - core if i < 4 else core) + lax.rem(y + i % 4, 4)

    def side(load_w, load_v, w_v, v_v, wt_s, wt_hbm, k, col, mask, hi_s, lo_s, hi_hbm, lo_hbm, out_s, sent, kept):
        load_w.wait()
        wt_s[...] = jnp.swapaxes(w_v[...], 0, 1)
        outs.append(copy(wt_s, wt_hbm, bc_sem.at[k]))
        outs[-1].start()
        load_v.wait()
        hi_s[...] = jnp.swapaxes(v_v[...], 0, 1)
        for i in range(G):
            g = order(i)
            spread = expander(g)
            scale = dot(col[...], spread)
            e_last = dot(et_s[T - 16 :, :], spread)[15:16]
            hi, lo = split2(hi_s[g].astype(F32) * scale)
            hi_s[g], lo_s[g] = hi, lo
            w = jnp.transpose(wt_s[g] * mask)
            block = dot(w, hi) + dot(w, lo)
            out_s[i, :N, :] = block if k else block * e_last
            out_s[i, N:, :] = jnp.concatenate(
                [e_last * whole, first, last, e_last, jnp.zeros((4, W), F32)], axis=0
            )
            started = copy(out_s.at[i], (sent if i < 4 else kept).at[i % 4], st_sem.at[8 * k + i])
            started.start()
            outs.append(started)
        outs.append(copy(hi_s, hi_hbm, xd_sem.at[2 * k]))
        outs.append(copy(lo_s, lo_hbm, xd_sem.at[2 * k + 1]))
        start(*outs[-2:])

    outs[0].start()
    side(
        loads[3], loads[4], b_v, x_v, bt_s, bt_hbm, 0, qt_s, last_mask,
        xh_s, xl_s, xh_hbm, xl_hbm, f_s, fs_hbm, fk_hbm,
    )
    side(
        loads[5], loads[6], c_v, dy_v, ct_s, ct_hbm, 1, et_s, first_mask,
        dh_s, dl_s, dh_hbm, dl_hbm, r_s, rs_hbm, rk_hbm,
    )
    wait(*outs)


def summaries(dt, rate, seg, x, dy, b, c):
    big, thin, block = sds(G, T, W, dtype=BF16), sds(G, T, N, dtype=BF16), sds(4, ROWS, W)
    tall = pltpu.VMEM((G, T, W), BF16)
    return call(
        summary_kernel,
        (rate, dt, seg, x, dy, b, c),
        [HBM] * 7,
        [big] * 4 + [thin] * 2 + [sds(T, N, dtype=BF16)] + [block] * 4,
        [
            pltpu.SMEM((J, G), F32), pltpu.VMEM((G, J, T), F32), pltpu.VMEM((1, T), jnp.int32),
            pltpu.VMEM((T, G, W), BF16), pltpu.VMEM((T, G, W), BF16),
            pltpu.VMEM((T, G, N), BF16), pltpu.VMEM((T, G, N), BF16),
            pltpu.VMEM((G, T, N), BF16), pltpu.VMEM((G, T, N), BF16),
            tall, tall, tall, tall,
            pltpu.VMEM((G, ROWS, W), F32), pltpu.VMEM((G, ROWS, W), F32),
            pltpu.VMEM((32, T), F32), pltpu.VMEM((32, T), F32),
            pltpu.VMEM((T, N), BF16), pltpu.VMEM((T, N), BF16),
            pltpu.SemaphoreType.DMA((7,)), pltpu.SemaphoreType.DMA((3,)),
            pltpu.SemaphoreType.DMA((4,)), pltpu.SemaphoreType.DMA((16,)),
        ],
        "summaries",
        8000,
        60,
    )


def local_kernel(seg_ref, xh_ref, xl_ref, dh_ref, dl_ref, b_ref, c_ref, *refs):
    gc_ref, gb_ref = refs[-2:]
    seg_row = seg_ref[...].astype(F32)
    low = lows(token_rows(seg_row), seg_row).astype(F32)
    for g in range(G):
        xh, dh = xh_ref[g], dh_ref[g]
        sums = dot_t(dh, xh) + dot_t(dh, xl_ref[g]) + dot_t(dl_ref[g], xh)
        sh, sl = split2(sums * low)
        gc_ref[g] = dot(sh, b_ref[g]) + dot(sl, b_ref[g])
        c_tr = jnp.transpose(c_ref[g])
        gb_ref[g] = jnp.transpose(dot(c_tr, sh) + dot(c_tr, sl))


def local_grads(seg, data, after):
    return call(
        local_kernel,
        (seg, *data, *after),
        [VMEM] * 7 + [HBM] * len(after),
        [sds(G, T, N)] * 2,
        [],
        "local_grads",
        3000,
        12,
        VMEM,
    )


def linked(earlier, later):
    return (earlier[LAST : LAST + 1, :] == later[FIRST : FIRST + 1, :]).astype(F32)


def join(earlier, later, out, rev):
    link = linked(earlier, later)
    near, far = (earlier, later) if rev else (later, earlier)
    out[:N, :] = near[:N, :] + (near[DEC : DEC + 1, :] * link) * far[:N, :]
    both = earlier[DEC : DEC + 1, :] * later[DEC : DEC + 1, :] * link
    out[N:, :] = jnp.concatenate(
        [both, earlier[FIRST : FIRST + 1, :], later[LAST : LAST + 1, :], jnp.zeros((5, W), F32)], axis=0
    )


def load_all(pairs, sems):
    loads = [copy(source, target, sems.at[k]) for k, (source, target) in enumerate(pairs)]
    start(*loads)
    return loads


def block(*lead):
    return pltpu.VMEM((*lead, ROWS, W), F32)


def sems(count):
    return pltpu.SemaphoreType.DMA((count,))


def small_call(body, args, after, outs, scratch, name):
    def kernel(*refs):
        body(*refs[: len(args)], *refs[len(args) + len(after) :])

    specs = [VMEM] * len(args) + [HBM] * len(after)
    return call(kernel, (*args, *after), specs, outs, scratch, name, 1000, 8, VMEM)


def chip_join(kept, got, rev, after=()):
    def body(kept, got, *outs):
        def go(earlier, later):
            for s in range(4):
                join(earlier.at[s], later.at[s], outs[s], rev)

        pl.when(place()[0] == 0)(lambda: go(kept, got))
        pl.when(place()[0] == 1)(lambda: go(got, kept))

    return small_call(body, (kept, got), after, [sds(ROWS, W)] * 4, [], "chip_join")


def by_y(blocks, go):
    y = place()[1]
    for k in range(4):
        pl.when(y == k)(lambda k=k: go([blocks[(k - there) % 4] for there in range(4)], k))


def plane_join(blocks, rev, after=()):
    def body(*refs):
        blocks, out, one, two = refs[:4], refs[4], refs[5], refs[6]

        def go(order, _):
            join(order[0], order[1], one, rev)
            join(order[2], order[3], two, rev)
            join(one, two, out, rev)

        by_y(blocks, go)

    return small_call(body, blocks, after, [sds(ROWS, W)], [block(), block()], "plane_join")[0]


def plane_enter(blocks, near, far, rev, after=()):
    def body(*refs):
        blocks, near, far, outs = refs[:4], refs[4], refs[5], refs[6:]

        def link(one, two):
            return linked(two, one) if rev else linked(one, two)

        def go(order, y):
            first, ahead = (3, -1) if rev else (0, 1)
            carry = near[:N, :] + (near[DEC : DEC + 1, :] * link(far, near)) * far[:N, :]
            carry = link(near, order[first]) * carry
            for step in range(4):
                here = first + step * ahead
                outs[(here - y) % 4][...] = carry
                if step < 3:
                    one = order[here]
                    carry = link(one, order[here + ahead]) * (one[:N, :] + one[DEC : DEC + 1, :] * carry)

        by_y(blocks, go)

    return small_call(body, (*blocks, near, far), after, [sds(N, W)] * 4, [], "plane_enter")


def device_enter(entering, kept, got, rev, after=()):
    inner = 1 if rev else 0

    def body(*refs):
        entering, kept, got, mine, other = refs[:4], refs[4], refs[5], refs[6], refs[7]
        core, y, _ = place()

        def go(near, far, direct, passed):
            for s in range(4):
                k, slot = lax.rem(y + 4 - s, 4), (4 - s) % 4
                one, two = near.at[slot], far.at[slot]
                link = linked(two, one) if rev else linked(one, two)
                direct[k] = entering[s][...]
                passed[k] = link * (one[:N, :] + one[DEC : DEC + 1, :] * entering[s][...])

        pl.when(core == inner)(lambda: go(kept, got, mine, other))
        pl.when(core != inner)(lambda: go(got, kept, other, mine))

    args = (*entering, kept, got)
    return small_call(body, args, after, [sds(4, N, W)] * 2, [], "device_enter")


def ring(count, shift):
    return [(i, (i + shift) % count) for i in range(count)]


def swap(v):
    return lax.ppermute(v, C, ring(2, 1))


def along_y(v, shift):
    return lax.ppermute(v, Y, ring(4, shift))


def along_z(v, shift):
    return lax.ppermute(v, Z, ring(8, shift))


def along_x(v, shift):
    return lax.ppermute(v, X, ring(4, shift))


def of_half(core, g, mine, got):
    return jnp.where(core == g // 4, mine[g % 4], got[g % 4])


def reverse_block(core, y, g, kept, sent, rows):
    slot = lax.rem(g % 4 + 4 - y, 4)
    return jnp.where(core == g // 4, kept[slot, rows, :], sent[slot, rows, :])


def sum_kernel(
    seg_ref, dh_ref, dl_ref, xh_ref, xl_ref, smine, sgot, amine, agot, kept, sent, gc_ref, gb_ref, *outs
):
    core, y, x = place()
    seg_t = token_rows(seg_ref[...].astype(F32))
    first, last = firsts(seg_t).astype(F32), lasts(seg_t).astype(F32)
    for i in range(G):
        g = lax.rem(2 * x + i, G)
        out, at = outs[i // 2], i % 2
        sh, sl = split2(of_half(core, g, smine, sgot))
        hi, lo = dh_ref[g], dl_ref[g]
        out[at] = gc_ref[g] + first * (dot_t(hi, sh) + dot_t(hi, sl) + dot_t(lo, sh))
        scale = reverse_block(core, y, g, kept, sent, slice(N, ROWS))[ELAST - N : ELAST - N + 1]
        ah, al = split2(of_half(core, g, amine, agot) * scale)
        hi, lo = xh_ref[g], xl_ref[g]
        out[2 + at] = gb_ref[g] + last * (dot_t(hi, ah) + dot_t(hi, al) + dot_t(lo, ah))


def summed(*args):
    return call(sum_kernel, args, [VMEM] * len(args), [sds(4, T, N)] * 4, [], "summed", 3000, 16, VMEM)


def token_kernel(
    rate, seg_ref, dt_ref, qt_ref, xh_ref, xl_ref, dh_ref, dl_ref, b_ref, c_ref,
    smine, sgot, amine, agot, kept, sent, *refs,
):
    gi_ref, gs_ref, gi_s, v_s, u_s, k_s, dt_s, rate_s = refs[-8:]
    core, y, _ = place()
    for j in range(J):
        for k in range(G):
            row = slice(J * k + j, J * k + j + 1)
            dt_s[row, :] = dt_ref[k, j : j + 1, :]
            rate_s[row, :] = jnp.full((1, T), rate[j, k], F32)
    seg_row = seg_ref[...].astype(F32)
    seg_t = token_rows(seg_row)
    first, last = firsts(seg_t).astype(BF16), lasts(seg_t).astype(BF16)
    low, high = lows(seg_t, seg_row).astype(F32), highs(seg_t, seg_row).astype(F32)
    ones = head_ones()
    for g in range(G):
        xh, xl, dh, dl, b, c = [ref[g] for ref in (xh_ref, xl_ref, dh_ref, dl_ref, b_ref, c_ref)]
        state, adjoint = of_half(core, g, smine, sgot), of_half(core, g, amine, agot)
        reverse = reverse_block(core, y, g, kept, sent, slice(0, ROWS))
        crossing = state * (reverse[:N] + reverse[DEC : DEC + 1] * adjoint)
        k_s[g] = head_sums(ones, crossing)
        sh, sl = split2(state)
        wh, wl = split2(dot_t(c, b) * low)
        edge = c * first
        out = dot(wh, xh) + dot(wh, xl) + dot(wl, xh) + dot(edge, sh) + dot(edge, sl)
        u_s[g] = head_sums(ones, out * (dh.astype(F32) + dl.astype(F32)))
        ah, al = split2(adjoint * reverse[ELAST : ELAST + 1])
        vh, vl = split2(dot_t(b, c) * high)
        edge = b * last
        raw = dot(vh, dh) + dot(vh, dl) + dot(vl, dh) + dot(edge, ah) + dot(edge, al)
        q = dot(qt_ref[...], expander(g))
        gi_s[g] = (q * raw).astype(BF16)
        v_s[g] = head_sums(ones, raw * (xh.astype(F32) + xl.astype(F32)))
    gi_ref[...] = jnp.swapaxes(gi_s[...], 0, 1)
    v = jnp.concatenate([v_s[k][:J] for k in range(G)], axis=0)
    u = jnp.concatenate([u_s[k][:J] for k in range(G)], axis=0)
    cross = jnp.concatenate([k_s[k][:J] for k in range(G)], axis=0)
    total = jnp.sum(cross, axis=1, keepdims=True)
    change = v - u + jnp.where(iota((32, T), 1) == 0, total, 0.0)
    run3 = dot_t(jnp.concatenate(split3(change), axis=0), lows(seg_t, seg_row).astype(BF16))
    inter = run3[:32] + run3[32:64] + run3[64:96] + u
    grad = v / dt_s[...] + rate_s[...] * (inter - v)
    for k in range(G):
        gs_ref[k] = grad[J * k : J * k + J]


def token_grads(args, after):
    args = (*args, *after)
    heads = pltpu.VMEM((G, 8, T), F32)
    return call(
        token_kernel,
        args,
        [SMEM] + [VMEM] * (len(args) - 1 - len(after)) + [HBM] * len(after),
        [sds(T, G, W, dtype=BF16), sds(G, J, T)],
        [
            pltpu.VMEM((G, T, W), BF16), heads, heads, pltpu.VMEM((G, 8, N), F32),
            pltpu.VMEM((32, T), F32), pltpu.VMEM((32, T), F32),
        ],
        "token_grads", 6000, 16, VMEM,
    )


def over_heads(parts):
    return [along_x(parts[s], s) for s in (1, 2, 3)]


def per_device(inputs, step_size, decay_rate, b_proj, c_proj, grad_out, segment_ids):
    seg = segment_ids.reshape(1, T)
    dt = jnp.transpose(step_size, (1, 2, 0))
    rate = jnp.transpose(decay_rate)
    xh, xl, dh, dl, b, c, qt, fs, fk, rs, rk = summaries(dt, rate, seg, inputs, grad_out, b_proj, c_proj)
    data = (xh, xl, dh, dl, b, c)

    def spread_y(blocks):
        return [blocks[0]] + [along_y(blocks[s], s) for s in (1, 2, 3)]

    fgot, rgot = swap(fs), swap(rs)
    fjoined = chip_join(fk, fgot, 0)
    rjoined = chip_join(rk, rgot, 1, (fjoined[0],))
    fblocks, rblocks = spread_y(fjoined), spread_y(rjoined)
    fplane = plane_join(fblocks, 0)
    rplane = plane_join(rblocks, 1, (fplane,))
    gc, gb = local_grads(seg, data, (rplane,))
    fenter = plane_enter(fblocks, along_z(fplane, 1), along_z(fplane, 2), 0, (gc,))
    renter = plane_enter(rblocks, along_z(rplane, -1), along_z(rplane, -2), 1, (fenter[0],))
    smine, fother = device_enter(spread_y(fenter), fk, fgot, 0)
    sgot = swap(fother)
    amine, rother = device_enter(spread_y(renter), rk, rgot, 1, (smine,))
    agot = swap(rother)
    parts = summed(seg, dh, dl, xh, xl, smine, sgot, amine, agot, rk, rs, gc, gb)
    got = over_heads(parts)
    grad_in, grad_step = token_grads(
        (rate, seg, dt, qt, xh, xl, dh, dl, b, c, smine, sgot, amine, agot, rk, rs), (parts[1],)
    )
    whole = parts[0] + got[0] + got[1] + got[2]
    total_c, total_b = jnp.transpose(whole[:2], (1, 0, 2)), jnp.transpose(whole[2:], (1, 0, 2))
    return grad_in, jnp.transpose(grad_step, (2, 0, 1)), total_b, total_c


def solution(mesh):
    fine = Mesh(mesh.devices.reshape(8, 4, 2, 4), (Z, Y, C, X))
    ctx = (Z, Y, C)
    placed = (
        P(ctx, None, X),
        P(ctx, None, X),
        P(None, X),
        P(ctx, None, None),
        P(ctx, None, None),
        P(ctx, None, X),
        P(ctx),
    )
    return jax.shard_map(
        per_device,
        mesh=fine,
        in_specs=placed,
        out_specs=(P(ctx, None, X), P(ctx, None, X), P(ctx, X, None), P(ctx, X, None)),
        check_vma=False,
    )
```

```python
import functools

import jax
import jax.numpy as jnp
from jax import lax
from jax.experimental import pallas as pl
from jax.experimental.pallas import tpu as pltpu
from jax.sharding import Mesh, PartitionSpec as P

F32 = jnp.float32
BF16 = jnp.bfloat16
T = 256
G = 8
J = 4
W = 256
N = 128
ROWS = N + 8
DEC, FIRST, LAST, ELAST = N, N + 1, N + 2, N + 3
HBM = pl.BlockSpec(memory_space=pltpu.HBM)
VMEM = pl.BlockSpec(memory_space=pltpu.VMEM)
SMEM = pl.BlockSpec(memory_space=pltpu.SMEM)
Z, Y, C, X = "z", "y", "core", "head"


def dot(a, b):
    return lax.dot_general(a, b, (((1,), (0,)), ((), ())), preferred_element_type=F32)


def dot_t(a, b):
    return lax.dot_general(a, b, (((1,), (1,)), ((), ())), preferred_element_type=F32)


def split2(v):
    hi = v.astype(BF16)
    return hi, (v - hi.astype(F32)).astype(BF16)


def split3(v):
    hi = v.astype(BF16)
    rest = v - hi.astype(F32)
    mid = rest.astype(BF16)
    return hi, mid, (rest - mid.astype(F32)).astype(BF16)


def iota(shape, dim):
    return lax.broadcasted_iota(jnp.int32, shape, dim)


def head_ones():
    return (iota((8, W), 0) == iota((8, W), 1) // 64).astype(BF16)


def expander(g):
    k = iota((128, W), 0)
    return ((k < 96) & (k % 32 == J * g + iota((128, W), 1) // 64)).astype(BF16)


def head_sums(ones, z):
    hi, lo = split2(z)
    return dot_t(ones, hi) + dot_t(ones, lo)


def token_rows(seg_row):
    padded = jnp.concatenate([seg_row, jnp.zeros((7, T), F32)], axis=0).astype(BF16)
    ones = jnp.ones((8, T), BF16)
    return lax.dot_general(padded, ones, (((0,), (0,)), ((), ())), preferred_element_type=F32)


def lows(seg_t, seg_row):
    return (seg_t == seg_row) & (iota((T, T), 1) <= iota((T, T), 0))


def highs(seg_t, seg_row):
    return (seg_t == seg_row) & (iota((T, T), 1) >= iota((T, T), 0))


def firsts(seg_t):
    return seg_t[:, :N] == seg_t[0:1, :N]


def lasts(seg_t):
    return seg_t[:, :N] == seg_t[T - 1 : T, :N]


def place():
    return lax.axis_index(C), lax.axis_index(Y), lax.axis_index(X)


def copy(source, target, sem):
    return pltpu.make_async_copy(source, target, sem)


def start(*copies):
    for one in copies:
        one.start()


def wait(*copies):
    for one in copies:
        one.wait()


def sds(*shape, dtype=F32):
    return jax.ShapeDtypeStruct(shape, dtype)


def call(kernel, args, specs, outs, scratch, name, mega, mib, out_spec=HBM, **more):
    return pl.pallas_call(
        kernel,
        in_specs=specs,
        out_specs=[out_spec] * len(outs),
        out_shape=outs,
        scratch_shapes=scratch,
        compiler_params=pltpu.CompilerParams(vmem_limit_bytes=mib * 2**20),
        cost_estimate=pl.CostEstimate(flops=mega * 10**3, bytes_accessed=2**10, transcendentals=0),
        name=name,
        **more,
    )(*args)


def columns(v):
    pieces = [piece.astype(F32) for piece in split3(v)] + [jnp.zeros((32, T), F32)]
    return jnp.transpose(jnp.concatenate(pieces, axis=0)).astype(BF16)


def summary_kernel(
    rate_hbm, dt_hbm, seg_hbm, x_hbm, dy_hbm, b_hbm, c_hbm,
    xh_hbm, xl_hbm, dh_hbm, dl_hbm, bt_hbm, ct_hbm, qt_hbm, fs_hbm, fk_hbm, rs_hbm, rk_hbm,
    rate, dt_v, seg_v, x_v, dy_v, b_v, c_v, bt_s, ct_s, xh_s, xl_s, dh_s, dl_s, f_s, r_s,
    a_s, dt_s, et_s, qt_s, in_sem, bc_sem, xd_sem, st_sem,
):
    core, y, _ = place()
    loads = [
        copy(source, target, in_sem.at[k])
        for k, (source, target) in enumerate(
            [
                (rate_hbm, rate), (dt_hbm, dt_v), (seg_hbm, seg_v),
                (b_hbm, b_v), (x_hbm, x_v), (c_hbm, c_v), (dy_hbm, dy_v),
            ]
        )
    ]
    start(*loads)
    wait(*loads[:3])
    for j in range(J):
        for k in range(G):
            row = slice(J * k + j, J * k + j + 1)
            dt_s[row, :] = dt_v[k, j : j + 1, :]
            a_s[row, :] = dt_v[k, j : j + 1, :] * rate[j, k]
    upto = (iota((T, T), 0) <= iota((T, T), 1)).astype(BF16)
    cum3 = dot(jnp.concatenate(split3(a_s[...]), axis=0), upto)
    cum = cum3[:32] + cum3[32:64] + cum3[64:96]
    et_s[...] = columns(jnp.exp(cum))
    qt_s[...] = columns(jnp.exp(-cum) * dt_s[...])
    seg_t = token_rows(seg_v[...].astype(F32))
    first_mask, last_mask = firsts(seg_t).astype(BF16), lasts(seg_t).astype(BF16)
    first, last = seg_t[0:1, :], seg_t[T - 1 : T, :]
    whole = (first == last).astype(F32)
    outs = [copy(qt_s, qt_hbm, bc_sem.at[2])]

    def order(i):
        return 4 * (1 - core if i < 4 else core) + lax.rem(y + i % 4, 4)

    def side(load_w, load_v, w_v, v_v, wt_s, wt_hbm, k, col, mask, hi_s, lo_s, hi_hbm, lo_hbm, out_s, sent, kept):
        load_w.wait()
        wt_s[...] = jnp.swapaxes(w_v[...], 0, 1)
        outs.append(copy(wt_s, wt_hbm, bc_sem.at[k]))
        outs[-1].start()
        load_v.wait()
        hi_s[...] = jnp.swapaxes(v_v[...], 0, 1)
        for i in range(G):
            g = order(i)
            spread = expander(g)
            scale = dot(col[...], spread)
            e_last = dot(et_s[T - 16 :, :], spread)[15:16]
            hi, lo = split2(hi_s[g].astype(F32) * scale)
            hi_s[g], lo_s[g] = hi, lo
            w = jnp.transpose(wt_s[g] * mask)
            block = dot(w, hi) + dot(w, lo)
            out_s[i, :N, :] = block if k else block * e_last
            out_s[i, N:, :] = jnp.concatenate(
                [e_last * whole, first, last, e_last, jnp.zeros((4, W), F32)], axis=0
            )
            started = copy(out_s.at[i], (sent if i < 4 else kept).at[i % 4], st_sem.at[8 * k + i])
            started.start()
            outs.append(started)
        outs.append(copy(hi_s, hi_hbm, xd_sem.at[2 * k]))
        outs.append(copy(lo_s, lo_hbm, xd_sem.at[2 * k + 1]))
        start(*outs[-2:])

    outs[0].start()
    side(
        loads[3], loads[4], b_v, x_v, bt_s, bt_hbm, 0, qt_s, last_mask,
        xh_s, xl_s, xh_hbm, xl_hbm, f_s, fs_hbm, fk_hbm,
    )
    side(
        loads[5], loads[6], c_v, dy_v, ct_s, ct_hbm, 1, et_s, first_mask,
        dh_s, dl_s, dh_hbm, dl_hbm, r_s, rs_hbm, rk_hbm,
    )
    wait(*outs)


def summaries(dt, rate, seg, x, dy, b, c):
    big, thin, block = sds(G, T, W, dtype=BF16), sds(G, T, N, dtype=BF16), sds(4, ROWS, W)
    tall = pltpu.VMEM((G, T, W), BF16)
    return call(
        summary_kernel,
        (rate, dt, seg, x, dy, b, c),
        [HBM] * 7,
        [big] * 4 + [thin] * 2 + [sds(T, N, dtype=BF16)] + [block] * 4,
        [
            pltpu.SMEM((J, G), F32), pltpu.VMEM((G, J, T), F32), pltpu.VMEM((1, T), jnp.int32),
            pltpu.VMEM((T, G, W), BF16), pltpu.VMEM((T, G, W), BF16),
            pltpu.VMEM((T, G, N), BF16), pltpu.VMEM((T, G, N), BF16),
            pltpu.VMEM((G, T, N), BF16), pltpu.VMEM((G, T, N), BF16),
            tall, tall, tall, tall,
            pltpu.VMEM((G, ROWS, W), F32), pltpu.VMEM((G, ROWS, W), F32),
            pltpu.VMEM((32, T), F32), pltpu.VMEM((32, T), F32),
            pltpu.VMEM((T, N), BF16), pltpu.VMEM((T, N), BF16),
            pltpu.SemaphoreType.DMA((7,)), pltpu.SemaphoreType.DMA((3,)),
            pltpu.SemaphoreType.DMA((4,)), pltpu.SemaphoreType.DMA((16,)),
        ],
        "summaries",
        8000,
        60,
    )


def local_kernel(seg_ref, xh_ref, xl_ref, dh_ref, dl_ref, b_ref, c_ref, *refs):
    gc_ref, gb_ref = refs[-2:]
    seg_row = seg_ref[...].astype(F32)
    low = lows(token_rows(seg_row), seg_row).astype(F32)
    for g in range(G):
        xh, dh = xh_ref[g], dh_ref[g]
        sums = dot_t(dh, xh) + dot_t(dh, xl_ref[g]) + dot_t(dl_ref[g], xh)
        sh, sl = split2(sums * low)
        gc_ref[g] = dot(sh, b_ref[g]) + dot(sl, b_ref[g])
        c_tr = jnp.transpose(c_ref[g])
        gb_ref[g] = jnp.transpose(dot(c_tr, sh) + dot(c_tr, sl))


def local_grads(seg, data, after):
    return call(
        local_kernel,
        (seg, *data, *after),
        [VMEM] * 7 + [HBM] * len(after),
        [sds(G, T, N)] * 2,
        [],
        "local_grads",
        3000,
        12,
        VMEM,
    )


def linked(earlier, later):
    return (earlier[LAST : LAST + 1, :] == later[FIRST : FIRST + 1, :]).astype(F32)


def join(earlier, later, out, rev):
    link = linked(earlier, later)
    near, far = (earlier, later) if rev else (later, earlier)
    out[:N, :] = near[:N, :] + (near[DEC : DEC + 1, :] * link) * far[:N, :]
    both = earlier[DEC : DEC + 1, :] * later[DEC : DEC + 1, :] * link
    out[N:, :] = jnp.concatenate(
        [both, earlier[FIRST : FIRST + 1, :], later[LAST : LAST + 1, :], jnp.zeros((5, W), F32)], axis=0
    )


def load_all(pairs, sems):
    loads = [copy(source, target, sems.at[k]) for k, (source, target) in enumerate(pairs)]
    start(*loads)
    return loads


def block(*lead):
    return pltpu.VMEM((*lead, ROWS, W), F32)


def sems(count):
    return pltpu.SemaphoreType.DMA((count,))


def small_call(body, args, after, outs, scratch, name):
    def kernel(*refs):
        body(*refs[: len(args)], *refs[len(args) + len(after) :])

    specs = [VMEM] * len(args) + [HBM] * len(after)
    return call(kernel, (*args, *after), specs, outs, scratch, name, 1000, 8, VMEM)


def chip_join(kept, got, rev, after=()):
    def body(kept, got, *outs):
        def go(earlier, later):
            for s in range(4):
                join(earlier.at[s], later.at[s], outs[s], rev)

        pl.when(place()[0] == 0)(lambda: go(kept, got))
        pl.when(place()[0] == 1)(lambda: go(got, kept))

    return small_call(body, (kept, got), after, [sds(ROWS, W)] * 4, [], "chip_join")


def by_y(blocks, go):
    y = place()[1]
    for k in range(4):
        pl.when(y == k)(lambda k=k: go([blocks[(k - there) % 4] for there in range(4)], k))


def plane_join(blocks, rev, after=()):
    def body(*refs):
        blocks, out, one, two = refs[:4], refs[4], refs[5], refs[6]

        def go(order, _):
            join(order[0], order[1], one, rev)
            join(order[2], order[3], two, rev)
            join(one, two, out, rev)

        by_y(blocks, go)

    return small_call(body, blocks, after, [sds(ROWS, W)], [block(), block()], "plane_join")[0]


def plane_enter(blocks, near, far, rev, after=()):
    def body(*refs):
        blocks, near, far, outs = refs[:4], refs[4], refs[5], refs[6:]

        def link(one, two):
            return linked(two, one) if rev else linked(one, two)

        def go(order, y):
            first, ahead = (3, -1) if rev else (0, 1)
            carry = near[:N, :] + (near[DEC : DEC + 1, :] * link(far, near)) * far[:N, :]
            carry = link(near, order[first]) * carry
            for step in range(4):
                here = first + step * ahead
                outs[(here - y) % 4][...] = carry
                if step < 3:
                    one = order[here]
                    carry = link(one, order[here + ahead]) * (one[:N, :] + one[DEC : DEC + 1, :] * carry)

        by_y(blocks, go)

    return small_call(body, (*blocks, near, far), after, [sds(N, W)] * 4, [], "plane_enter")


def device_enter(entering, kept, got, rev, after=()):
    inner = 1 if rev else 0

    def body(*refs):
        entering, kept, got, mine, other = refs[:4], refs[4], refs[5], refs[6], refs[7]
        core, y, _ = place()

        def go(near, far, direct, passed):
            for s in range(4):
                k, slot = lax.rem(y + 4 - s, 4), (4 - s) % 4
                one, two = near.at[slot], far.at[slot]
                link = linked(two, one) if rev else linked(one, two)
                direct[k] = entering[s][...]
                passed[k] = link * (one[:N, :] + one[DEC : DEC + 1, :] * entering[s][...])

        pl.when(core == inner)(lambda: go(kept, got, mine, other))
        pl.when(core != inner)(lambda: go(got, kept, other, mine))

    args = (*entering, kept, got)
    return small_call(body, args, after, [sds(4, N, W)] * 2, [], "device_enter")


def ring(count, shift):
    return [(i, (i + shift) % count) for i in range(count)]


def swap(v):
    return lax.ppermute(v, C, ring(2, 1))


def along_y(v, shift):
    return lax.ppermute(v, Y, ring(4, shift))


def along_z(v, shift):
    return lax.ppermute(v, Z, ring(8, shift))


def along_x(v, shift):
    return lax.ppermute(v, X, ring(4, shift))


def of_half(core, g, mine, got):
    return jnp.where(core == g // 4, mine[g % 4], got[g % 4])


def reverse_block(core, y, g, kept, sent, rows):
    slot = lax.rem(g % 4 + 4 - y, 4)
    return jnp.where(core == g // 4, kept[slot, rows, :], sent[slot, rows, :])


def sum_kernel(
    seg_ref, dh_ref, dl_ref, xh_ref, xl_ref, smine, sgot, amine, agot, kept, sent, gc_ref, gb_ref, *outs
):
    core, y, x = place()
    seg_t = token_rows(seg_ref[...].astype(F32))
    first, last = firsts(seg_t).astype(F32), lasts(seg_t).astype(F32)
    for i in range(G):
        g = lax.rem(2 * x + i, G)
        out, at = outs[i // 2], i % 2
        sh, sl = split2(of_half(core, g, smine, sgot))
        hi, lo = dh_ref[g], dl_ref[g]
        out[at] = gc_ref[g] + first * (dot_t(hi, sh) + dot_t(hi, sl) + dot_t(lo, sh))
        scale = reverse_block(core, y, g, kept, sent, slice(N, ROWS))[ELAST - N : ELAST - N + 1]
        ah, al = split2(of_half(core, g, amine, agot) * scale)
        hi, lo = xh_ref[g], xl_ref[g]
        out[2 + at] = gb_ref[g] + last * (dot_t(hi, ah) + dot_t(hi, al) + dot_t(lo, ah))


def summed(*args):
    return call(sum_kernel, args, [VMEM] * len(args), [sds(4, T, N)] * 4, [], "summed", 3000, 16, VMEM)


def token_kernel(
    rate, seg_ref, dt_ref, qt_ref, xh_ref, xl_ref, dh_ref, dl_ref, b_ref, c_ref,
    smine, sgot, amine, agot, kept, sent, *refs,
):
    gi_ref, gs_ref, gi_s, v_s, u_s, k_s, dt_s, rate_s = refs[-8:]
    core, y, _ = place()
    for j in range(J):
        for k in range(G):
            row = slice(J * k + j, J * k + j + 1)
            dt_s[row, :] = dt_ref[k, j : j + 1, :]
            rate_s[row, :] = jnp.full((1, T), rate[j, k], F32)
    seg_row = seg_ref[...].astype(F32)
    seg_t = token_rows(seg_row)
    first, last = firsts(seg_t).astype(BF16), lasts(seg_t).astype(BF16)
    low, high = lows(seg_t, seg_row).astype(F32), highs(seg_t, seg_row).astype(F32)
    ones = head_ones()
    for g in range(G):
        xh, xl, dh, dl, b, c = [ref[g] for ref in (xh_ref, xl_ref, dh_ref, dl_ref, b_ref, c_ref)]
        state, adjoint = of_half(core, g, smine, sgot), of_half(core, g, amine, agot)
        reverse = reverse_block(core, y, g, kept, sent, slice(0, ROWS))
        crossing = state * (reverse[:N] + reverse[DEC : DEC + 1] * adjoint)
        k_s[g] = head_sums(ones, crossing)
        sh, sl = split2(state)
        wh, wl = split2(dot_t(c, b) * low)
        edge = c * first
        out = dot(wh, xh) + dot(wh, xl) + dot(wl, xh) + dot(edge, sh) + dot(edge, sl)
        u_s[g] = head_sums(ones, out * (dh.astype(F32) + dl.astype(F32)))
        ah, al = split2(adjoint * reverse[ELAST : ELAST + 1])
        vh, vl = split2(dot_t(b, c) * high)
        edge = b * last
        raw = dot(vh, dh) + dot(vh, dl) + dot(vl, dh) + dot(edge, ah) + dot(edge, al)
        q = dot(qt_ref[...], expander(g))
        gi_s[g] = (q * raw).astype(BF16)
        v_s[g] = head_sums(ones, raw * (xh.astype(F32) + xl.astype(F32)))
    gi_ref[...] = jnp.swapaxes(gi_s[...], 0, 1)
    v = jnp.concatenate([v_s[k][:J] for k in range(G)], axis=0)
    u = jnp.concatenate([u_s[k][:J] for k in range(G)], axis=0)
    cross = jnp.concatenate([k_s[k][:J] for k in range(G)], axis=0)
    total = jnp.sum(cross, axis=1, keepdims=True)
    change = v - u + jnp.where(iota((32, T), 1) == 0, total, 0.0)
    run3 = dot_t(jnp.concatenate(split3(change), axis=0), lows(seg_t, seg_row).astype(BF16))
    inter = run3[:32] + run3[32:64] + run3[64:96] + u
    grad = v / dt_s[...] + rate_s[...] * (inter - v)
    for k in range(G):
        gs_ref[k] = grad[J * k : J * k + J]


def token_grads(args, after):
    args = (*args, *after)
    heads = pltpu.VMEM((G, 8, T), F32)
    return call(
        token_kernel,
        args,
        [SMEM] + [VMEM] * (len(args) - 1 - len(after)) + [HBM] * len(after),
        [sds(T, G, W, dtype=BF16), sds(G, J, T)],
        [
            pltpu.VMEM((G, T, W), BF16), heads, heads, pltpu.VMEM((G, 8, N), F32),
            pltpu.VMEM((32, T), F32), pltpu.VMEM((32, T), F32),
        ],
        "token_grads", 6000, 16, VMEM,
    )


def over_heads(parts):
    return [along_x(parts[s], s) for s in (1, 2, 3)]


def finish(parts):
    def body(*refs):
        parts, outs = refs[:4], refs[4:]
        for k in range(2):
            own = slice(2 * k, 2 * k + 2)
            whole = parts[0][own] + parts[1][own] + parts[2][own] + parts[3][own]
            outs[k][...] = jnp.swapaxes(whole, 0, 1)

    return call(body, parts, [VMEM] * 4, [sds(T, 2, N)] * 2, [], "finish", 1, 12, VMEM)


def per_device(inputs, step_size, decay_rate, b_proj, c_proj, grad_out, segment_ids):
    seg = segment_ids.reshape(1, T)
    dt = jnp.transpose(step_size, (1, 2, 0))
    rate = jnp.transpose(decay_rate)
    xh, xl, dh, dl, b, c, qt, fs, fk, rs, rk = summaries(dt, rate, seg, inputs, grad_out, b_proj, c_proj)
    data = (xh, xl, dh, dl, b, c)

    def spread_y(blocks):
        return [blocks[0]] + [along_y(blocks[s], s) for s in (1, 2, 3)]

    fgot, rgot = swap(fs), swap(rs)
    fjoined = chip_join(fk, fgot, 0)
    rjoined = chip_join(rk, rgot, 1, (fjoined[0],))
    fblocks, rblocks = spread_y(fjoined), spread_y(rjoined)
    fplane = plane_join(fblocks, 0)
    rplane = plane_join(rblocks, 1, (fplane,))
    fenter = plane_enter(fblocks, along_z(fplane, 1), along_z(fplane, 2), 0)
    renter = plane_enter(rblocks, along_z(rplane, -1), along_z(rplane, -2), 1, (fenter[0],))
    gc, gb = local_grads(seg, data, (renter[0],))
    smine, fother = device_enter(spread_y(fenter), fk, fgot, 0)
    sgot = swap(fother)
    amine, rother = device_enter(spread_y(renter), rk, rgot, 1, (smine, gc))
    agot = swap(rother)
    parts = summed(seg, dh, dl, xh, xl, smine, sgot, amine, agot, rk, rs, gc, gb)
    got = over_heads(parts)
    grad_in, grad_step = token_grads(
        (rate, seg, dt, qt, xh, xl, dh, dl, b, c, smine, sgot, amine, agot, rk, rs), (parts[1],)
    )
    total_c, total_b = finish((parts[0], *got))
    return grad_in, jnp.transpose(grad_step, (2, 0, 1)), total_b, total_c


def solution(mesh):
    fine = Mesh(mesh.devices.reshape(8, 4, 2, 4), (Z, Y, C, X))
    ctx = (Z, Y, C)
    placed = (
        P(ctx, None, X),
        P(ctx, None, X),
        P(None, X),
        P(ctx, None, None),
        P(ctx, None, None),
        P(ctx, None, X),
        P(ctx),
    )
    return jax.shard_map(
        per_device,
        mesh=fine,
        in_specs=placed,
        out_specs=(P(ctx, None, X), P(ctx, None, X), P(ctx, X, None), P(ctx, X, None)),
        check_vma=False,
    )
```

```python
import functools

import jax
import jax.numpy as jnp
from jax import lax
from jax.experimental import pallas as pl
from jax.experimental.pallas import tpu as pltpu
from jax.sharding import Mesh, PartitionSpec as P

F32 = jnp.float32
BF16 = jnp.bfloat16
T = 256
G = 8
J = 4
W = 256
N = 128
ROWS = N + 8
DEC, FIRST, LAST, ELAST = N, N + 1, N + 2, N + 3
HBM = pl.BlockSpec(memory_space=pltpu.HBM)
VMEM = pl.BlockSpec(memory_space=pltpu.VMEM)
SMEM = pl.BlockSpec(memory_space=pltpu.SMEM)
Z, Y, C, X = "z", "y", "core", "head"


def dot(a, b):
    return lax.dot_general(a, b, (((1,), (0,)), ((), ())), preferred_element_type=F32)


def dot_t(a, b):
    return lax.dot_general(a, b, (((1,), (1,)), ((), ())), preferred_element_type=F32)


def split2(v):
    hi = v.astype(BF16)
    return hi, (v - hi.astype(F32)).astype(BF16)


def split3(v):
    hi = v.astype(BF16)
    rest = v - hi.astype(F32)
    mid = rest.astype(BF16)
    return hi, mid, (rest - mid.astype(F32)).astype(BF16)


def iota(shape, dim):
    return lax.broadcasted_iota(jnp.int32, shape, dim)


def head_ones():
    return (iota((8, W), 0) == iota((8, W), 1) // 64).astype(BF16)


def expander(g):
    k = iota((128, W), 0)
    return ((k < 96) & (k % 32 == J * g + iota((128, W), 1) // 64)).astype(BF16)


def head_sums(ones, z):
    hi, lo = split2(z)
    return dot_t(ones, hi) + dot_t(ones, lo)


def token_rows(seg_row):
    padded = jnp.concatenate([seg_row, jnp.zeros((7, T), F32)], axis=0).astype(BF16)
    ones = jnp.ones((8, T), BF16)
    return lax.dot_general(padded, ones, (((0,), (0,)), ((), ())), preferred_element_type=F32)


def lows(seg_t, seg_row):
    return (seg_t == seg_row) & (iota((T, T), 1) <= iota((T, T), 0))


def highs(seg_t, seg_row):
    return (seg_t == seg_row) & (iota((T, T), 1) >= iota((T, T), 0))


def firsts(seg_t):
    return seg_t[:, :N] == seg_t[0:1, :N]


def lasts(seg_t):
    return seg_t[:, :N] == seg_t[T - 1 : T, :N]


def place():
    return lax.axis_index(C), lax.axis_index(Y), lax.axis_index(X)


def copy(source, target, sem):
    return pltpu.make_async_copy(source, target, sem)


def start(*copies):
    for one in copies:
        one.start()


def wait(*copies):
    for one in copies:
        one.wait()


def sds(*shape, dtype=F32):
    return jax.ShapeDtypeStruct(shape, dtype)


def call(kernel, args, specs, outs, scratch, name, mega, mib, out_spec=HBM, **more):
    return pl.pallas_call(
        kernel,
        in_specs=specs,
        out_specs=[out_spec] * len(outs),
        out_shape=outs,
        scratch_shapes=scratch,
        compiler_params=pltpu.CompilerParams(vmem_limit_bytes=mib * 2**20),
        cost_estimate=pl.CostEstimate(flops=mega * 10**3, bytes_accessed=2**10, transcendentals=0),
        name=name,
        **more,
    )(*args)


def columns(v):
    pieces = [piece.astype(F32) for piece in split3(v)] + [jnp.zeros((32, T), F32)]
    return jnp.transpose(jnp.concatenate(pieces, axis=0)).astype(BF16)


def summary_kernel(
    rate_hbm, dt_hbm, seg_hbm, x_hbm, dy_hbm, b_hbm, c_hbm,
    xh_hbm, xl_hbm, dh_hbm, dl_hbm, bt_hbm, ct_hbm, qt_hbm, fs_hbm, fk_hbm, rs_hbm, rk_hbm,
    rate, dt_v, seg_v, x_v, dy_v, b_v, c_v, bt_s, ct_s, xh_s, xl_s, dh_s, dl_s, f_s, r_s,
    a_s, dt_s, et_s, qt_s, in_sem, bc_sem, xd_sem, st_sem,
):
    core, y, _ = place()
    loads = [
        copy(source, target, in_sem.at[k])
        for k, (source, target) in enumerate(
            [
                (rate_hbm, rate), (dt_hbm, dt_v), (seg_hbm, seg_v),
                (b_hbm, b_v), (x_hbm, x_v), (c_hbm, c_v), (dy_hbm, dy_v),
            ]
        )
    ]
    start(*loads)
    wait(*loads[:3])
    for j in range(J):
        for k in range(G):
            row = slice(J * k + j, J * k + j + 1)
            dt_s[row, :] = dt_v[k, j : j + 1, :]
            a_s[row, :] = dt_v[k, j : j + 1, :] * rate[j, k]
    upto = (iota((T, T), 0) <= iota((T, T), 1)).astype(BF16)
    cum3 = dot(jnp.concatenate(split3(a_s[...]), axis=0), upto)
    cum = cum3[:32] + cum3[32:64] + cum3[64:96]
    et_s[...] = columns(jnp.exp(cum))
    qt_s[...] = columns(jnp.exp(-cum) * dt_s[...])
    seg_t = token_rows(seg_v[...].astype(F32))
    first_mask, last_mask = firsts(seg_t).astype(BF16), lasts(seg_t).astype(BF16)
    first, last = seg_t[0:1, :], seg_t[T - 1 : T, :]
    whole = (first == last).astype(F32)
    outs = [copy(qt_s, qt_hbm, bc_sem.at[2])]

    def order(i):
        return 4 * (1 - core if i < 4 else core) + lax.rem(y + i % 4, 4)

    def side(load_w, load_v, w_v, v_v, wt_s, wt_hbm, k, col, mask, hi_s, lo_s, hi_hbm, lo_hbm, out_s, sent, kept):
        load_w.wait()
        wt_s[...] = jnp.swapaxes(w_v[...], 0, 1)
        outs.append(copy(wt_s, wt_hbm, bc_sem.at[k]))
        outs[-1].start()
        load_v.wait()
        hi_s[...] = jnp.swapaxes(v_v[...], 0, 1)
        for i in range(G):
            g = order(i)
            spread = expander(g)
            scale = dot(col[...], spread)
            e_last = dot(et_s[T - 16 :, :], spread)[15:16]
            hi, lo = split2(hi_s[g].astype(F32) * scale)
            hi_s[g], lo_s[g] = hi, lo
            w = jnp.transpose(wt_s[g] * mask)
            block = dot(w, hi) + dot(w, lo)
            out_s[i, :N, :] = block if k else block * e_last
            out_s[i, N:, :] = jnp.concatenate(
                [e_last * whole, first, last, e_last, jnp.zeros((4, W), F32)], axis=0
            )
            started = copy(out_s.at[i], (sent if i < 4 else kept).at[i % 4], st_sem.at[8 * k + i])
            started.start()
            outs.append(started)
        outs.append(copy(hi_s, hi_hbm, xd_sem.at[2 * k]))
        outs.append(copy(lo_s, lo_hbm, xd_sem.at[2 * k + 1]))
        start(*outs[-2:])

    outs[0].start()
    side(
        loads[3], loads[4], b_v, x_v, bt_s, bt_hbm, 0, qt_s, last_mask,
        xh_s, xl_s, xh_hbm, xl_hbm, f_s, fs_hbm, fk_hbm,
    )
    side(
        loads[5], loads[6], c_v, dy_v, ct_s, ct_hbm, 1, et_s, first_mask,
        dh_s, dl_s, dh_hbm, dl_hbm, r_s, rs_hbm, rk_hbm,
    )
    wait(*outs)


def summaries(dt, rate, seg, x, dy, b, c):
    big, thin, block = sds(G, T, W, dtype=BF16), sds(G, T, N, dtype=BF16), sds(4, ROWS, W)
    tall = pltpu.VMEM((G, T, W), BF16)
    return call(
        summary_kernel,
        (rate, dt, seg, x, dy, b, c),
        [HBM] * 7,
        [big] * 4 + [thin] * 2 + [sds(T, N, dtype=BF16)] + [block] * 4,
        [
            pltpu.SMEM((J, G), F32), pltpu.VMEM((G, J, T), F32), pltpu.VMEM((1, T), jnp.int32),
            pltpu.VMEM((T, G, W), BF16), pltpu.VMEM((T, G, W), BF16),
            pltpu.VMEM((T, G, N), BF16), pltpu.VMEM((T, G, N), BF16),
            pltpu.VMEM((G, T, N), BF16), pltpu.VMEM((G, T, N), BF16),
            tall, tall, tall, tall,
            pltpu.VMEM((G, ROWS, W), F32), pltpu.VMEM((G, ROWS, W), F32),
            pltpu.VMEM((32, T), F32), pltpu.VMEM((32, T), F32),
            pltpu.VMEM((T, N), BF16), pltpu.VMEM((T, N), BF16),
            pltpu.SemaphoreType.DMA((7,)), pltpu.SemaphoreType.DMA((3,)),
            pltpu.SemaphoreType.DMA((4,)), pltpu.SemaphoreType.DMA((16,)),
        ],
        "summaries",
        8000,
        60,
    )


def local_kernel(seg_ref, xh_ref, xl_ref, dh_ref, dl_ref, b_ref, c_ref, *refs):
    gc_ref, gb_ref = refs[-2:]
    seg_row = seg_ref[...].astype(F32)
    low = lows(token_rows(seg_row), seg_row).astype(F32)
    for g in range(G):
        xh, dh = xh_ref[g], dh_ref[g]
        sums = dot_t(dh, xh) + dot_t(dh, xl_ref[g]) + dot_t(dl_ref[g], xh)
        sh, sl = split2(sums * low)
        gc_ref[g] = dot(sh, b_ref[g]) + dot(sl, b_ref[g])
        c_tr = jnp.transpose(c_ref[g])
        gb_ref[g] = jnp.transpose(dot(c_tr, sh) + dot(c_tr, sl))


def local_grads(seg, data, after):
    return call(
        local_kernel,
        (seg, *data, *after),
        [VMEM] * 7 + [HBM] * len(after),
        [sds(G, T, N)] * 2,
        [],
        "local_grads",
        3000,
        12,
        VMEM,
    )


def linked(earlier, later):
    return (earlier[LAST : LAST + 1, :] == later[FIRST : FIRST + 1, :]).astype(F32)


def join(earlier, later, out, rev):
    link = linked(earlier, later)
    near, far = (earlier, later) if rev else (later, earlier)
    out[:N, :] = near[:N, :] + (near[DEC : DEC + 1, :] * link) * far[:N, :]
    both = earlier[DEC : DEC + 1, :] * later[DEC : DEC + 1, :] * link
    out[N:, :] = jnp.concatenate(
        [both, earlier[FIRST : FIRST + 1, :], later[LAST : LAST + 1, :], jnp.zeros((5, W), F32)], axis=0
    )


def load_all(pairs, sems):
    loads = [copy(source, target, sems.at[k]) for k, (source, target) in enumerate(pairs)]
    start(*loads)
    return loads


def block(*lead):
    return pltpu.VMEM((*lead, ROWS, W), F32)


def sems(count):
    return pltpu.SemaphoreType.DMA((count,))


def small_call(body, args, after, outs, scratch, name):
    def kernel(*refs):
        body(*refs[: len(args)], *refs[len(args) + len(after) :])

    specs = [VMEM] * len(args) + [HBM] * len(after)
    return call(kernel, (*args, *after), specs, outs, scratch, name, 1000, 8, VMEM)


def chip_join(kept, got, rev, after=()):
    def body(kept, got, *outs):
        def go(earlier, later):
            for s in range(4):
                join(earlier.at[s], later.at[s], outs[s], rev)

        pl.when(place()[0] == 0)(lambda: go(kept, got))
        pl.when(place()[0] == 1)(lambda: go(got, kept))

    return small_call(body, (kept, got), after, [sds(ROWS, W)] * 4, [], "chip_join")


def by_y(blocks, go):
    y = place()[1]
    for k in range(4):
        pl.when(y == k)(lambda k=k: go([blocks[(k - there) % 4] for there in range(4)], k))


def plane_join(blocks, rev, after=()):
    def body(*refs):
        blocks, out, one, two = refs[:4], refs[4], refs[5], refs[6]

        def go(order, _):
            join(order[0], order[1], one, rev)
            join(order[2], order[3], two, rev)
            join(one, two, out, rev)

        by_y(blocks, go)

    return small_call(body, blocks, after, [sds(ROWS, W)], [block(), block()], "plane_join")[0]


def plane_enter(blocks, near, far, rev, after=()):
    def body(*refs):
        blocks, near, far, outs = refs[:4], refs[4], refs[5], refs[6:]

        def link(one, two):
            return linked(two, one) if rev else linked(one, two)

        def go(order, y):
            first, ahead = (3, -1) if rev else (0, 1)
            carry = near[:N, :] + (near[DEC : DEC + 1, :] * link(far, near)) * far[:N, :]
            carry = link(near, order[first]) * carry
            for step in range(4):
                here = first + step * ahead
                outs[(here - y) % 4][...] = carry
                if step < 3:
                    one = order[here]
                    carry = link(one, order[here + ahead]) * (one[:N, :] + one[DEC : DEC + 1, :] * carry)

        by_y(blocks, go)

    return small_call(body, (*blocks, near, far), after, [sds(N, W)] * 4, [], "plane_enter")


def device_enter(entering, kept, got, rev, after=()):
    inner = 1 if rev else 0

    def body(*refs):
        entering, kept, got, mine, other = refs[:4], refs[4], refs[5], refs[6], refs[7]
        core, y, _ = place()

        def go(near, far, direct, passed):
            for s in range(4):
                k, slot = lax.rem(y + 4 - s, 4), (4 - s) % 4
                one, two = near.at[slot], far.at[slot]
                link = linked(two, one) if rev else linked(one, two)
                direct[k] = entering[s][...]
                passed[k] = link * (one[:N, :] + one[DEC : DEC + 1, :] * entering[s][...])

        pl.when(core == inner)(lambda: go(kept, got, mine, other))
        pl.when(core != inner)(lambda: go(got, kept, other, mine))

    args = (*entering, kept, got)
    return small_call(body, args, after, [sds(4, N, W)] * 2, [], "device_enter")


def ring(count, shift):
    return [(i, (i + shift) % count) for i in range(count)]


def swap(v):
    return lax.ppermute(v, C, ring(2, 1))


def along_y(v, shift):
    return lax.ppermute(v, Y, ring(4, shift))


def along_z(v, shift):
    return lax.ppermute(v, Z, ring(8, shift))


def along_x(v, shift):
    return lax.ppermute(v, X, ring(4, shift))


def of_half(core, g, mine, got):
    return jnp.where(core == g // 4, mine[g % 4], got[g % 4])


def reverse_block(core, y, g, kept, sent, rows):
    slot = lax.rem(g % 4 + 4 - y, 4)
    return jnp.where(core == g // 4, kept[slot, rows, :], sent[slot, rows, :])


def sum_kernel(
    seg_ref, dh_ref, dl_ref, xh_ref, xl_ref, smine, sgot, amine, agot, kept, sent, gc_ref, gb_ref, *outs
):
    core, y, x = place()
    seg_t = token_rows(seg_ref[...].astype(F32))
    first, last = firsts(seg_t).astype(F32), lasts(seg_t).astype(F32)
    for i in range(G):
        g = lax.rem(2 * x + i, G)
        out_c, out_b, at = outs[i // 2], outs[4 + i // 2], i % 2
        sh, sl = split2(of_half(core, g, smine, sgot))
        hi, lo = dh_ref[g], dl_ref[g]
        out_c[at] = gc_ref[g] + first * (dot_t(hi, sh) + dot_t(hi, sl) + dot_t(lo, sh))
        scale = reverse_block(core, y, g, kept, sent, slice(N, ROWS))[ELAST - N : ELAST - N + 1]
        ah, al = split2(of_half(core, g, amine, agot) * scale)
        hi, lo = xh_ref[g], xl_ref[g]
        out_b[at] = gb_ref[g] + last * (dot_t(hi, ah) + dot_t(hi, al) + dot_t(lo, ah))


def summed(*args):
    return call(sum_kernel, args, [VMEM] * len(args), [sds(2, T, N)] * 8, [], "summed", 3000, 16, VMEM)


def token_kernel(
    rate, seg_ref, dt_ref, qt_ref, xh_ref, xl_ref, dh_ref, dl_ref, b_ref, c_ref,
    smine, sgot, amine, agot, kept, sent, *refs,
):
    gi_ref, gs_ref, gi_s, v_s, u_s, k_s, dt_s, rate_s = refs[-8:]
    core, y, _ = place()
    for j in range(J):
        for k in range(G):
            row = slice(J * k + j, J * k + j + 1)
            dt_s[row, :] = dt_ref[k, j : j + 1, :]
            rate_s[row, :] = jnp.full((1, T), rate[j, k], F32)
    seg_row = seg_ref[...].astype(F32)
    seg_t = token_rows(seg_row)
    first, last = firsts(seg_t).astype(BF16), lasts(seg_t).astype(BF16)
    low, high = lows(seg_t, seg_row).astype(F32), highs(seg_t, seg_row).astype(F32)
    ones = head_ones()
    for g in range(G):
        xh, xl, dh, dl, b, c = [ref[g] for ref in (xh_ref, xl_ref, dh_ref, dl_ref, b_ref, c_ref)]
        state, adjoint = of_half(core, g, smine, sgot), of_half(core, g, amine, agot)
        reverse = reverse_block(core, y, g, kept, sent, slice(0, ROWS))
        crossing = state * (reverse[:N] + reverse[DEC : DEC + 1] * adjoint)
        k_s[g] = head_sums(ones, crossing)
        sh, sl = split2(state)
        wh, wl = split2(dot_t(c, b) * low)
        edge = c * first
        out = dot(wh, xh) + dot(wh, xl) + dot(wl, xh) + dot(edge, sh) + dot(edge, sl)
        u_s[g] = head_sums(ones, out * (dh.astype(F32) + dl.astype(F32)))
        ah, al = split2(adjoint * reverse[ELAST : ELAST + 1])
        vh, vl = split2(dot_t(b, c) * high)
        edge = b * last
        raw = dot(vh, dh) + dot(vh, dl) + dot(vl, dh) + dot(edge, ah) + dot(edge, al)
        q = dot(qt_ref[...], expander(g))
        gi_s[g] = (q * raw).astype(BF16)
        v_s[g] = head_sums(ones, raw * (xh.astype(F32) + xl.astype(F32)))
    gi_ref[...] = jnp.swapaxes(gi_s[...], 0, 1)
    v = jnp.concatenate([v_s[k][:J] for k in range(G)], axis=0)
    u = jnp.concatenate([u_s[k][:J] for k in range(G)], axis=0)
    cross = jnp.concatenate([k_s[k][:J] for k in range(G)], axis=0)
    total = jnp.sum(cross, axis=1, keepdims=True)
    change = v - u + jnp.where(iota((32, T), 1) == 0, total, 0.0)
    run3 = dot_t(jnp.concatenate(split3(change), axis=0), lows(seg_t, seg_row).astype(BF16))
    inter = run3[:32] + run3[32:64] + run3[64:96] + u
    grad = v / dt_s[...] + rate_s[...] * (inter - v)
    for k in range(G):
        gs_ref[k] = grad[J * k : J * k + J]


def token_grads(args, after):
    args = (*args, *after)
    heads = pltpu.VMEM((G, 8, T), F32)
    return call(
        token_kernel,
        args,
        [SMEM] + [VMEM] * (len(args) - 1 - len(after)) + [HBM] * len(after),
        [sds(T, G, W, dtype=BF16), sds(G, J, T)],
        [
            pltpu.VMEM((G, T, W), BF16), heads, heads, pltpu.VMEM((G, 8, N), F32),
            pltpu.VMEM((32, T), F32), pltpu.VMEM((32, T), F32),
        ],
        "token_grads", 6000, 16, VMEM,
    )


def finish(own_c, own_b, *more):
    def body(*refs):
        for k in range(2):
            whole = refs[k][...] + refs[2 + k][...] + refs[4 + k][...]
            refs[6 + k][...] = jnp.swapaxes(whole, 0, 1)

    args = (own_c, own_b, *more)
    return call(body, args, [VMEM] * 6, [sds(T, 2, N)] * 2, [], "finish", 1, 12, VMEM)


def add_passed(one, one_got, two, two_got, after):
    def body(one, one_got, two, two_got, *refs):
        refs[-2][...] = one[...] + one_got[...]
        refs[-1][...] = two[...] + two_got[...]

    specs = [VMEM] * 4 + [HBM] * len(after)
    args = (one, one_got, two, two_got, *after)
    return call(body, args, specs, [sds(2, T, N)] * 2, [], "add_passed", 1, 12, VMEM)


def per_device(inputs, step_size, decay_rate, b_proj, c_proj, grad_out, segment_ids):
    seg = segment_ids.reshape(1, T)
    dt = jnp.transpose(step_size, (1, 2, 0))
    rate = jnp.transpose(decay_rate)
    xh, xl, dh, dl, b, c, qt, fs, fk, rs, rk = summaries(dt, rate, seg, inputs, grad_out, b_proj, c_proj)
    data = (xh, xl, dh, dl, b, c)

    def spread_y(blocks):
        return [blocks[0]] + [along_y(blocks[s], s) for s in (1, 2, 3)]

    fgot, rgot = swap(fs), swap(rs)
    fjoined = chip_join(fk, fgot, 0)
    rjoined = chip_join(rk, rgot, 1, (fjoined[0],))
    fblocks, rblocks = spread_y(fjoined), spread_y(rjoined)
    fplane = plane_join(fblocks, 0)
    rplane = plane_join(rblocks, 1, (fplane,))
    fenter = plane_enter(fblocks, along_z(fplane, 1), along_z(fplane, 2), 0)
    renter = plane_enter(rblocks, along_z(rplane, -1), along_z(rplane, -2), 1, (fenter[0],))
    gc, gb = local_grads(seg, data, (renter[0],))
    smine, fother = device_enter(spread_y(fenter), fk, fgot, 0)
    sgot = swap(fother)
    amine, rother = device_enter(spread_y(renter), rk, rgot, 1, (smine, gc))
    agot = swap(rother)
    parts = summed(seg, dh, dl, xh, xl, smine, sgot, amine, agot, rk, rs, gc, gb)
    cs, bs = parts[:4], parts[4:]
    c_passed, b_passed = along_x(cs[2], 1), along_x(bs[2], 3)
    b_before, c_behind = along_x(bs[1], 1), along_x(cs[3], 3)
    grad_in, grad_step = token_grads(
        (rate, seg, dt, qt, xh, xl, dh, dl, b, c, smine, sgot, amine, agot, rk, rs), (parts[1],)
    )
    c_sent, b_sent = add_passed(cs[1], c_passed, bs[3], b_passed, (grad_step,))
    c_before, b_behind = along_x(c_sent, 1), along_x(b_sent, 3)
    total_c, total_b = finish(cs[0], bs[0], c_before, b_before, c_behind, b_behind)
    return grad_in, jnp.transpose(grad_step, (2, 0, 1)), total_b, total_c


def solution(mesh):
    fine = Mesh(mesh.devices.reshape(8, 4, 2, 4), (Z, Y, C, X))
    ctx = (Z, Y, C)
    placed = (
        P(ctx, None, X),
        P(ctx, None, X),
        P(None, X),
        P(ctx, None, None),
        P(ctx, None, None),
        P(ctx, None, X),
        P(ctx),
    )
    return jax.shard_map(
        per_device,
        mesh=fine,
        in_specs=placed,
        out_specs=(P(ctx, None, X), P(ctx, None, X), P(ctx, X, None), P(ctx, X, None)),
        check_vma=False,
    )
```

```python
import functools

import jax
import jax.numpy as jnp
from jax import lax
from jax.experimental import pallas as pl
from jax.experimental.pallas import tpu as pltpu
from jax.sharding import Mesh, PartitionSpec as P

F32 = jnp.float32
BF16 = jnp.bfloat16
T = 256
G = 8
J = 4
W = 256
N = 128
ROWS = N + 8
DEC, FIRST, LAST, ELAST = N, N + 1, N + 2, N + 3
HBM = pl.BlockSpec(memory_space=pltpu.HBM)
VMEM = pl.BlockSpec(memory_space=pltpu.VMEM)
SMEM = pl.BlockSpec(memory_space=pltpu.SMEM)
Z, Y, C, X = "z", "y", "core", "head"


def dot(a, b):
    return lax.dot_general(a, b, (((1,), (0,)), ((), ())), preferred_element_type=F32)


def dot_t(a, b):
    return lax.dot_general(a, b, (((1,), (1,)), ((), ())), preferred_element_type=F32)


def split2(v):
    hi = v.astype(BF16)
    return hi, (v - hi.astype(F32)).astype(BF16)


def split3(v):
    hi = v.astype(BF16)
    rest = v - hi.astype(F32)
    mid = rest.astype(BF16)
    return hi, mid, (rest - mid.astype(F32)).astype(BF16)


def iota(shape, dim):
    return lax.broadcasted_iota(jnp.int32, shape, dim)


def head_ones():
    return (iota((8, W), 0) == iota((8, W), 1) // 64).astype(BF16)


def expander(g):
    k = iota((128, W), 0)
    return ((k < 96) & (k % 32 == J * g + iota((128, W), 1) // 64)).astype(BF16)


def head_sums(ones, z):
    hi, lo = split2(z)
    return dot_t(ones, hi) + dot_t(ones, lo)


def token_rows(seg_row):
    padded = jnp.concatenate([seg_row, jnp.zeros((7, T), F32)], axis=0).astype(BF16)
    ones = jnp.ones((8, T), BF16)
    return lax.dot_general(padded, ones, (((0,), (0,)), ((), ())), preferred_element_type=F32)


def lows(seg_t, seg_row):
    return (seg_t == seg_row) & (iota((T, T), 1) <= iota((T, T), 0))


def highs(seg_t, seg_row):
    return (seg_t == seg_row) & (iota((T, T), 1) >= iota((T, T), 0))


def firsts(seg_t):
    return seg_t[:, :N] == seg_t[0:1, :N]


def lasts(seg_t):
    return seg_t[:, :N] == seg_t[T - 1 : T, :N]


def place():
    return lax.axis_index(C), lax.axis_index(Y), lax.axis_index(X)


def copy(source, target, sem):
    return pltpu.make_async_copy(source, target, sem)


def start(*copies):
    for one in copies:
        one.start()


def wait(*copies):
    for one in copies:
        one.wait()


def sds(*shape, dtype=F32):
    return jax.ShapeDtypeStruct(shape, dtype)


def call(kernel, args, specs, outs, scratch, name, mega, mib, out_spec=HBM, **more):
    return pl.pallas_call(
        kernel,
        in_specs=specs,
        out_specs=[out_spec] * len(outs),
        out_shape=outs,
        scratch_shapes=scratch,
        compiler_params=pltpu.CompilerParams(vmem_limit_bytes=mib * 2**20),
        cost_estimate=pl.CostEstimate(flops=mega * 10**5, bytes_accessed=2**10, transcendentals=0),
        name=name,
        **more,
    )(*args)


def columns(v):
    pieces = [piece.astype(F32) for piece in split3(v)] + [jnp.zeros((32, T), F32)]
    return jnp.transpose(jnp.concatenate(pieces, axis=0)).astype(BF16)


def summary_kernel(
    rate_hbm, dt_hbm, seg_hbm, x_hbm, dy_hbm, b_hbm, c_hbm,
    xh_hbm, xl_hbm, dh_hbm, dl_hbm, bt_hbm, ct_hbm, qt_hbm, fs_hbm, fk_hbm, rs_hbm, rk_hbm,
    rate, dt_v, seg_v, x_v, dy_v, b_v, c_v, bt_s, ct_s, xh_s, xl_s, dh_s, dl_s, f_s, r_s,
    a_s, dt_s, et_s, qt_s, in_sem, bc_sem, xd_sem, st_sem,
):
    core, y, _ = place()
    loads = [
        copy(source, target, in_sem.at[k])
        for k, (source, target) in enumerate(
            [
                (rate_hbm, rate), (dt_hbm, dt_v), (seg_hbm, seg_v),
                (b_hbm, b_v), (x_hbm, x_v), (c_hbm, c_v), (dy_hbm, dy_v),
            ]
        )
    ]
    start(*loads)
    wait(*loads[:3])
    for j in range(J):
        for k in range(G):
            row = slice(J * k + j, J * k + j + 1)
            dt_s[row, :] = dt_v[k, j : j + 1, :]
            a_s[row, :] = dt_v[k, j : j + 1, :] * rate[j, k]
    upto = (iota((T, T), 0) <= iota((T, T), 1)).astype(BF16)
    cum3 = dot(jnp.concatenate(split3(a_s[...]), axis=0), upto)
    cum = cum3[:32] + cum3[32:64] + cum3[64:96]
    et_s[...] = columns(jnp.exp(cum))
    qt_s[...] = columns(jnp.exp(-cum) * dt_s[...])
    seg_t = token_rows(seg_v[...].astype(F32))
    first_mask, last_mask = firsts(seg_t).astype(BF16), lasts(seg_t).astype(BF16)
    first, last = seg_t[0:1, :], seg_t[T - 1 : T, :]
    whole = (first == last).astype(F32)
    outs = [copy(qt_s, qt_hbm, bc_sem.at[2])]

    def order(i):
        return 4 * (1 - core if i < 4 else core) + lax.rem(y + i % 4, 4)

    def side(load_w, load_v, w_v, v_v, wt_s, wt_hbm, k, col, mask, hi_s, lo_s, hi_hbm, lo_hbm, out_s, sent, kept):
        load_w.wait()
        wt_s[...] = jnp.swapaxes(w_v[...], 0, 1)
        outs.append(copy(wt_s, wt_hbm, bc_sem.at[k]))
        outs[-1].start()
        load_v.wait()
        hi_s[...] = jnp.swapaxes(v_v[...], 0, 1)
        for i in range(G):
            g = order(i)
            spread = expander(g)
            scale = dot(col[...], spread)
            e_last = dot(et_s[T - 16 :, :], spread)[15:16]
            hi, lo = split2(hi_s[g].astype(F32) * scale)
            hi_s[g], lo_s[g] = hi, lo
            w = jnp.transpose(wt_s[g] * mask)
            block = dot(w, hi) + dot(w, lo)
            out_s[i, :N, :] = block if k else block * e_last
            out_s[i, N:, :] = jnp.concatenate(
                [e_last * whole, first, last, e_last, jnp.zeros((4, W), F32)], axis=0
            )
            started = copy(out_s.at[i], (sent if i < 4 else kept).at[i % 4], st_sem.at[8 * k + i])
            started.start()
            outs.append(started)
        outs.append(copy(hi_s, hi_hbm, xd_sem.at[2 * k]))
        outs.append(copy(lo_s, lo_hbm, xd_sem.at[2 * k + 1]))
        start(*outs[-2:])

    outs[0].start()
    side(
        loads[3], loads[4], b_v, x_v, bt_s, bt_hbm, 0, qt_s, last_mask,
        xh_s, xl_s, xh_hbm, xl_hbm, f_s, fs_hbm, fk_hbm,
    )
    side(
        loads[5], loads[6], c_v, dy_v, ct_s, ct_hbm, 1, et_s, first_mask,
        dh_s, dl_s, dh_hbm, dl_hbm, r_s, rs_hbm, rk_hbm,
    )
    wait(*outs)


def summaries(dt, rate, seg, x, dy, b, c):
    big, thin, block = sds(G, T, W, dtype=BF16), sds(G, T, N, dtype=BF16), sds(4, ROWS, W)
    tall = pltpu.VMEM((G, T, W), BF16)
    return call(
        summary_kernel,
        (rate, dt, seg, x, dy, b, c),
        [HBM] * 7,
        [big] * 4 + [thin] * 2 + [sds(T, N, dtype=BF16)] + [block] * 4,
        [
            pltpu.SMEM((J, G), F32), pltpu.VMEM((G, J, T), F32), pltpu.VMEM((1, T), jnp.int32),
            pltpu.VMEM((T, G, W), BF16), pltpu.VMEM((T, G, W), BF16),
            pltpu.VMEM((T, G, N), BF16), pltpu.VMEM((T, G, N), BF16),
            pltpu.VMEM((G, T, N), BF16), pltpu.VMEM((G, T, N), BF16),
            tall, tall, tall, tall,
            pltpu.VMEM((G, ROWS, W), F32), pltpu.VMEM((G, ROWS, W), F32),
            pltpu.VMEM((32, T), F32), pltpu.VMEM((32, T), F32),
            pltpu.VMEM((T, N), BF16), pltpu.VMEM((T, N), BF16),
            pltpu.SemaphoreType.DMA((7,)), pltpu.SemaphoreType.DMA((3,)),
            pltpu.SemaphoreType.DMA((4,)), pltpu.SemaphoreType.DMA((16,)),
        ],
        "summaries",
        8000,
        60,
    )


def local_kernel(seg_ref, xh_ref, xl_ref, dh_ref, dl_ref, b_ref, c_ref, *refs):
    gc_ref, gb_ref = refs[-2:]
    seg_row = seg_ref[...].astype(F32)
    low = lows(token_rows(seg_row), seg_row).astype(F32)
    for g in range(G):
        xh, dh = xh_ref[g], dh_ref[g]
        sums = dot_t(dh, xh) + dot_t(dh, xl_ref[g]) + dot_t(dl_ref[g], xh)
        sh, sl = split2(sums * low)
        gc_ref[g] = dot(sh, b_ref[g]) + dot(sl, b_ref[g])
        c_tr = jnp.transpose(c_ref[g])
        gb_ref[g] = jnp.transpose(dot(c_tr, sh) + dot(c_tr, sl))


def local_grads(seg, data, after):
    return call(
        local_kernel,
        (seg, *data, *after),
        [VMEM] * 7 + [HBM] * len(after),
        [sds(G, T, N)] * 2,
        [],
        "local_grads",
        3000,
        12,
        VMEM,
    )


def linked(earlier, later):
    return (earlier[LAST : LAST + 1, :] == later[FIRST : FIRST + 1, :]).astype(F32)


def join(earlier, later, out, rev):
    link = linked(earlier, later)
    near, far = (earlier, later) if rev else (later, earlier)
    out[:N, :] = near[:N, :] + (near[DEC : DEC + 1, :] * link) * far[:N, :]
    both = earlier[DEC : DEC + 1, :] * later[DEC : DEC + 1, :] * link
    out[N:, :] = jnp.concatenate(
        [both, earlier[FIRST : FIRST + 1, :], later[LAST : LAST + 1, :], jnp.zeros((5, W), F32)], axis=0
    )


def load_all(pairs, sems):
    loads = [copy(source, target, sems.at[k]) for k, (source, target) in enumerate(pairs)]
    start(*loads)
    return loads


def block(*lead):
    return pltpu.VMEM((*lead, ROWS, W), F32)


def sems(count):
    return pltpu.SemaphoreType.DMA((count,))


def small_call(body, args, after, outs, scratch, name):
    def kernel(*refs):
        body(*refs[: len(args)], *refs[len(args) + len(after) :])

    specs = [VMEM] * len(args) + [HBM] * len(after)
    return call(kernel, (*args, *after), specs, outs, scratch, name, 1000, 8, VMEM)


def chip_join(kept, got, rev, after=()):
    def body(kept, got, *outs):
        def go(earlier, later):
            for s in range(4):
                join(earlier.at[s], later.at[s], outs[s], rev)

        pl.when(place()[0] == 0)(lambda: go(kept, got))
        pl.when(place()[0] == 1)(lambda: go(got, kept))

    return small_call(body, (kept, got), after, [sds(ROWS, W)] * 4, [], "chip_join")


def by_y(blocks, go):
    y = place()[1]
    for k in range(4):
        pl.when(y == k)(lambda k=k: go([blocks[(k - there) % 4] for there in range(4)], k))


def plane_join(blocks, rev, after=()):
    def body(*refs):
        blocks, out, one, two = refs[:4], refs[4], refs[5], refs[6]

        def go(order, _):
            join(order[0], order[1], one, rev)
            join(order[2], order[3], two, rev)
            join(one, two, out, rev)

        by_y(blocks, go)

    return small_call(body, blocks, after, [sds(ROWS, W)], [block(), block()], "plane_join")[0]


def plane_enter(blocks, near, far, rev, after=()):
    def body(*refs):
        blocks, near, far, outs = refs[:4], refs[4], refs[5], refs[6:]

        def link(one, two):
            return linked(two, one) if rev else linked(one, two)

        def go(order, y):
            first, ahead = (3, -1) if rev else (0, 1)
            carry = near[:N, :] + (near[DEC : DEC + 1, :] * link(far, near)) * far[:N, :]
            carry = link(near, order[first]) * carry
            for step in range(4):
                here = first + step * ahead
                outs[(here - y) % 4][...] = carry
                if step < 3:
                    one = order[here]
                    carry = link(one, order[here + ahead]) * (one[:N, :] + one[DEC : DEC + 1, :] * carry)

        by_y(blocks, go)

    return small_call(body, (*blocks, near, far), after, [sds(N, W)] * 4, [], "plane_enter")


def device_enter(entering, kept, got, rev, after=()):
    inner = 1 if rev else 0

    def body(*refs):
        entering, kept, got, mine, other = refs[:4], refs[4], refs[5], refs[6], refs[7]
        core, y, _ = place()

        def go(near, far, direct, passed):
            for s in range(4):
                k, slot = lax.rem(y + 4 - s, 4), (4 - s) % 4
                one, two = near.at[slot], far.at[slot]
                link = linked(two, one) if rev else linked(one, two)
                direct[k] = entering[s][...]
                passed[k] = link * (one[:N, :] + one[DEC : DEC + 1, :] * entering[s][...])

        pl.when(core == inner)(lambda: go(kept, got, mine, other))
        pl.when(core != inner)(lambda: go(got, kept, other, mine))

    args = (*entering, kept, got)
    return small_call(body, args, after, [sds(4, N, W)] * 2, [], "device_enter")


def ring(count, shift):
    return [(i, (i + shift) % count) for i in range(count)]


def swap(v):
    return lax.ppermute(v, C, ring(2, 1))


def along_y(v, shift):
    return lax.ppermute(v, Y, ring(4, shift))


def along_z(v, shift):
    return lax.ppermute(v, Z, ring(8, shift))


def along_x(v, shift):
    return lax.ppermute(v, X, ring(4, shift))


def of_half(core, g, mine, got):
    return jnp.where(core == g // 4, mine[g % 4], got[g % 4])


def reverse_block(core, y, g, kept, sent, rows):
    slot = lax.rem(g % 4 + 4 - y, 4)
    return jnp.where(core == g // 4, kept[slot, rows, :], sent[slot, rows, :])


def sum_kernel(
    seg_ref, dh_ref, dl_ref, xh_ref, xl_ref, smine, sgot, amine, agot, kept, sent, gc_ref, gb_ref, *outs
):
    core, y, x = place()
    seg_t = token_rows(seg_ref[...].astype(F32))
    first, last = firsts(seg_t).astype(F32), lasts(seg_t).astype(F32)
    for i in range(G):
        g = lax.rem(2 * x + i, G)
        out, at = outs[i // 2], i % 2
        sh, sl = split2(of_half(core, g, smine, sgot))
        hi, lo = dh_ref[g], dl_ref[g]
        out[at] = gc_ref[g] + first * (dot_t(hi, sh) + dot_t(hi, sl) + dot_t(lo, sh))
        scale = reverse_block(core, y, g, kept, sent, slice(N, ROWS))[ELAST - N : ELAST - N + 1]
        ah, al = split2(of_half(core, g, amine, agot) * scale)
        hi, lo = xh_ref[g], xl_ref[g]
        out[2 + at] = gb_ref[g] + last * (dot_t(hi, ah) + dot_t(hi, al) + dot_t(lo, ah))


def summed(*args):
    return call(sum_kernel, args, [VMEM] * len(args), [sds(4, T, N)] * 4, [], "summed", 3000, 16, VMEM)


def token_kernel(
    rate, seg_ref, dt_ref, qt_ref, xh_ref, xl_ref, dh_ref, dl_ref, b_ref, c_ref,
    smine, sgot, amine, agot, kept, sent, *refs,
):
    gi_ref, gs_ref, gi_s, v_s, u_s, k_s, dt_s, rate_s = refs[-8:]
    core, y, _ = place()
    for j in range(J):
        for k in range(G):
            row = slice(J * k + j, J * k + j + 1)
            dt_s[row, :] = dt_ref[k, j : j + 1, :]
            rate_s[row, :] = jnp.full((1, T), rate[j, k], F32)
    seg_row = seg_ref[...].astype(F32)
    seg_t = token_rows(seg_row)
    first, last = firsts(seg_t).astype(BF16), lasts(seg_t).astype(BF16)
    low, high = lows(seg_t, seg_row).astype(F32), highs(seg_t, seg_row).astype(F32)
    ones = head_ones()
    for g in range(G):
        xh, xl, dh, dl, b, c = [ref[g] for ref in (xh_ref, xl_ref, dh_ref, dl_ref, b_ref, c_ref)]
        state, adjoint = of_half(core, g, smine, sgot), of_half(core, g, amine, agot)
        reverse = reverse_block(core, y, g, kept, sent, slice(0, ROWS))
        crossing = state * (reverse[:N] + reverse[DEC : DEC + 1] * adjoint)
        k_s[g] = head_sums(ones, crossing)
        sh, sl = split2(state)
        wh, wl = split2(dot_t(c, b) * low)
        edge = c * first
        out = dot(wh, xh) + dot(wh, xl) + dot(wl, xh) + dot(edge, sh) + dot(edge, sl)
        u_s[g] = head_sums(ones, out * (dh.astype(F32) + dl.astype(F32)))
        ah, al = split2(adjoint * reverse[ELAST : ELAST + 1])
        vh, vl = split2(dot_t(b, c) * high)
        edge = b * last
        raw = dot(vh, dh) + dot(vh, dl) + dot(vl, dh) + dot(edge, ah) + dot(edge, al)
        q = dot(qt_ref[...], expander(g))
        gi_s[g] = (q * raw).astype(BF16)
        v_s[g] = head_sums(ones, raw * (xh.astype(F32) + xl.astype(F32)))
    gi_ref[...] = jnp.swapaxes(gi_s[...], 0, 1)
    v = jnp.concatenate([v_s[k][:J] for k in range(G)], axis=0)
    u = jnp.concatenate([u_s[k][:J] for k in range(G)], axis=0)
    cross = jnp.concatenate([k_s[k][:J] for k in range(G)], axis=0)
    total = jnp.sum(cross, axis=1, keepdims=True)
    change = v - u + jnp.where(iota((32, T), 1) == 0, total, 0.0)
    run3 = dot_t(jnp.concatenate(split3(change), axis=0), lows(seg_t, seg_row).astype(BF16))
    inter = run3[:32] + run3[32:64] + run3[64:96] + u
    grad = v / dt_s[...] + rate_s[...] * (inter - v)
    for k in range(G):
        gs_ref[k] = grad[J * k : J * k + J]


def token_grads(args, after):
    args = (*args, *after)
    heads = pltpu.VMEM((G, 8, T), F32)
    return call(
        token_kernel,
        args,
        [SMEM] + [VMEM] * (len(args) - 1 - len(after)) + [HBM] * len(after),
        [sds(T, G, W, dtype=BF16), sds(G, J, T)],
        [
            pltpu.VMEM((G, T, W), BF16), heads, heads, pltpu.VMEM((G, 8, N), F32),
            pltpu.VMEM((32, T), F32), pltpu.VMEM((32, T), F32),
        ],
        "token_grads", 6000, 16, VMEM,
    )


def over_heads(parts):
    return [along_x(parts[s], s) for s in (1, 2, 3)]


def finish(parts):
    def body(*refs):
        parts, outs = refs[:4], refs[4:]
        for k in range(2):
            own = slice(2 * k, 2 * k + 2)
            whole = parts[0][own] + parts[1][own] + parts[2][own] + parts[3][own]
            outs[k][...] = jnp.swapaxes(whole, 0, 1)

    return call(body, parts, [VMEM] * 4, [sds(T, 2, N)] * 2, [], "finish", 1, 12, VMEM)


def per_device(inputs, step_size, decay_rate, b_proj, c_proj, grad_out, segment_ids):
    seg = segment_ids.reshape(1, T)
    dt = jnp.transpose(step_size, (1, 2, 0))
    rate = jnp.transpose(decay_rate)
    xh, xl, dh, dl, b, c, qt, fs, fk, rs, rk = summaries(dt, rate, seg, inputs, grad_out, b_proj, c_proj)
    data = (xh, xl, dh, dl, b, c)

    def spread_y(blocks):
        return [blocks[0]] + [along_y(blocks[s], s) for s in (1, 2, 3)]

    fgot, rgot = swap(fs), swap(rs)
    fjoined = chip_join(fk, fgot, 0)
    rjoined = chip_join(rk, rgot, 1, (fjoined[0],))
    fblocks, rblocks = spread_y(fjoined), spread_y(rjoined)
    fplane = plane_join(fblocks, 0)
    rplane = plane_join(rblocks, 1, (fplane,))
    fenter = plane_enter(fblocks, along_z(fplane, 1), along_z(fplane, 2), 0)
    renter = plane_enter(rblocks, along_z(rplane, -1), along_z(rplane, -2), 1, (fenter[0],))
    gc, gb = local_grads(seg, data, (renter[0],))
    smine, fother = device_enter(spread_y(fenter), fk, fgot, 0)
    sgot = swap(fother)
    amine, rother = device_enter(spread_y(renter), rk, rgot, 1, (smine, gc))
    agot = swap(rother)
    parts = summed(seg, dh, dl, xh, xl, smine, sgot, amine, agot, rk, rs, gc, gb)
    got = over_heads(parts)
    grad_in, grad_step = token_grads(
        (rate, seg, dt, qt, xh, xl, dh, dl, b, c, smine, sgot, amine, agot, rk, rs), (parts[1],)
    )
    total_c, total_b = finish((parts[0], *got))
    return grad_in, jnp.transpose(grad_step, (2, 0, 1)), total_b, total_c


def solution(mesh):
    fine = Mesh(mesh.devices.reshape(8, 4, 2, 4), (Z, Y, C, X))
    ctx = (Z, Y, C)
    placed = (
        P(ctx, None, X),
        P(ctx, None, X),
        P(None, X),
        P(ctx, None, None),
        P(ctx, None, None),
        P(ctx, None, X),
        P(ctx),
    )
    return jax.shard_map(
        per_device,
        mesh=fine,
        in_specs=placed,
        out_specs=(P(ctx, None, X), P(ctx, None, X), P(ctx, X, None), P(ctx, X, None)),
        check_vma=False,
    )
```
